32 devices in a mesh: row: 4 (over x, core), col: 2 (over y), layer: 4 (over z).
Axes of the slice: x: 2, y: 2, z: 4, core: 2. Of those that a mesh axis runs over, the one named last changes fastest.
Arguments:
- a_values: float32 [4, 2, 4, 2, 8, 64, 64], P('row', 'col', 'layer'), may hold values from -6 to 6
- a_places: int32 [4, 2, 4, 2, 8, 2], P('row', 'col', 'layer'), may hold values from 0 to 7, as said below
- a_counts: int32 [4, 2, 4, 2], P('row', 'col', 'layer'), may hold values from 2 to 8, as said below
- b_values: float32 [4, 2, 4, 24, 64, 64], P('row', 'col', 'layer'), may hold values from -0.375 to 0.375
- b_places: int32 [4, 2, 4, 24, 2], P('row', 'col', 'layer'), may hold values from 0 to 15, as said below
- b_counts: int32 [4, 2, 4], P('row', 'col', 'layer'), may hold values from 6 to 24, as said below
Outputs:
- product: float32 [2048, 2048], P(('row', 'layer'), 'col')
The draws below stay inside these ranges and needn't reach their ends.
Inputs may be any that keep to these rules, and one draw needn't show every extreme that they name: a_places[..., 0] lies below 8 and a_places[..., 1] below 2; within one tile the slots name distinct positions. b_places[..., 0] lies below 2 and b_places[..., 1] below 16; within one tile the slots name distinct positions. `a_counts`: some tile is full. `b_counts`: some tile is full.
All inputs are finite; a program needn't handle non-finite values.
Results may differ from the reference program's by a relative error of at most 0.00007.
Values sent between devices are 32-bit elements; how exact they have to be, the bound alone decides.
A program may use at most 64 MiB of HBM per device.

```python
import jax
import jax.numpy as jnp
from jax import lax

BLOCK = 64
TILE_ROWS = 8
NBLOCKS = 32
TILE_INNER = 2
TILE_COLS = 16
CYCLE_SLOTS = 2
CAP_A = 8
CAP_B = 24
N_ROW = 4
N_COL = 2
N_LAYER = 4


def distinct_places(key, tiles, rows, cols, capacity):
    total = rows * cols
    scores = jax.random.randint(key, (tiles, total), 0, 65536, dtype=jnp.int32)
    scores = scores * total + jnp.arange(total, dtype=jnp.int32)[None, :]
    order = jnp.argsort(scores, axis=1)[:, :capacity].astype(jnp.int32)
    return jnp.stack([order // cols, order % cols], axis=-1)


def tile_counts(key, tiles, capacity):
    first, second = jax.random.split(key)
    counts = jax.random.randint(first, (tiles,), max(1, capacity // 4), capacity + 1, dtype=jnp.int32)
    chosen = jax.random.randint(second, (), 0, tiles, dtype=jnp.int32)
    return jnp.where(jnp.arange(tiles, dtype=jnp.int32) == chosen, capacity, counts)


def draw_a_places(key, part):
    key = jax.random.fold_in(key, 11)
    tiles = N_ROW * N_COL * N_LAYER * CYCLE_SLOTS
    places = distinct_places(key, tiles, TILE_ROWS, TILE_INNER, CAP_A)
    return places.reshape(N_ROW, N_COL, N_LAYER, CYCLE_SLOTS, CAP_A, 2)


def draw_a_counts(key, part):
    key = jax.random.fold_in(key, 23)
    tiles = N_ROW * N_COL * N_LAYER * CYCLE_SLOTS
    return tile_counts(key, tiles, CAP_A).reshape(N_ROW, N_COL, N_LAYER, CYCLE_SLOTS)


def draw_b_places(key, part):
    key = jax.random.fold_in(key, 37)
    tiles = N_ROW * N_COL * N_LAYER
    places = distinct_places(key, tiles, TILE_INNER, TILE_COLS, CAP_B)
    return places.reshape(N_ROW, N_COL, N_LAYER, CAP_B, 2)


def draw_b_counts(key, part):
    key = jax.random.fold_in(key, 41)
    tiles = N_ROW * N_COL * N_LAYER
    return tile_counts(key, tiles, CAP_B).reshape(N_ROW, N_COL, N_LAYER)


def shard_levels(own_key, extent, cuts, low, high):
    loudness, own = 1.0, jax.random.fold_in(own_key, 6)
    for dim, parts in cuts:
        steps = jnp.exp(jax.random.uniform(jax.random.fold_in(own, dim), (parts,), jnp.float32, low / len(cuts), high / len(cuts)))
        loudness = loudness * jnp.repeat(steps, extent[dim] // parts).reshape([-1 if axis == dim else 1 for axis in range(len(extent))])
    return loudness


def bell_draw(stream_key, extent, scale, limit, cuts=(), held_as=jnp.bfloat16):
    level = shard_levels(stream_key, extent, cuts, -0.22, 0.18) if cuts else 1.0
    array = jax.random.normal(stream_key, extent, jnp.float32) * scale * level
    return jnp.minimum(jnp.maximum(array, -limit), limit).astype(held_as)


def setup_inputs(seed: int = 0) -> dict:
    splits = jax.random.split(jax.random.key(seed), 7)
    a_values = bell_draw(splits[0], (N_ROW, N_COL, N_LAYER, CYCLE_SLOTS, CAP_A, BLOCK, BLOCK), 1.0, 6.0, ((0, 4), (1, 2), (2, 4)), jnp.float32)
    a_places = draw_a_places(jax.random.fold_in(splits[6], 71), 0)
    a_counts = draw_a_counts(jax.random.fold_in(splits[6], 71), 0)
    b_values = bell_draw(splits[3], (N_ROW, N_COL, N_LAYER, CAP_B, BLOCK, BLOCK), (NBLOCKS * BLOCK // 8) ** -0.5, 0.375, ((0, 4), (1, 2), (2, 4)), jnp.float32)
    b_places = draw_b_places(jax.random.fold_in(splits[6], 71), 0)
    b_counts = draw_b_counts(jax.random.fold_in(splits[6], 71), 0)
    return dict(a_values=a_values, a_places=a_places, a_counts=a_counts, b_values=b_values, b_places=b_places, b_counts=b_counts)


def place_blocks(values, block_rows, block_cols, live):
    zero = jnp.zeros((), values.dtype)
    flat_vals = jnp.where(live[..., None, None], values, zero).reshape(-1, BLOCK, BLOCK)
    grid = jnp.zeros((NBLOCKS, NBLOCKS, BLOCK, BLOCK), values.dtype)
    grid = grid.at[block_rows.reshape(-1), block_cols.reshape(-1)].add(flat_vals)
    return grid.transpose(0, 2, 1, 3).reshape(NBLOCKS * BLOCK, NBLOCKS * BLOCK)


def reference(a_values, a_places, a_counts, b_values, b_places, b_counts):
    row_ids = jnp.arange(N_ROW, dtype=jnp.int32).reshape(-1, 1, 1, 1)
    col_ids = jnp.arange(N_COL, dtype=jnp.int32).reshape(1, -1, 1, 1)
    layer_ids = jnp.arange(N_LAYER, dtype=jnp.int32).reshape(1, 1, -1, 1)
    slot_ids = jnp.arange(CYCLE_SLOTS, dtype=jnp.int32).reshape(1, 1, 1, -1)
    piece_a = N_ROW * layer_ids + (row_ids + col_ids + N_COL * slot_ids) % N_ROW
    rows_a = row_ids[..., None] * TILE_ROWS + a_places[..., 0]
    cols_a = piece_a[..., None] * TILE_INNER + a_places[..., 1]
    live_a = jnp.arange(CAP_A, dtype=jnp.int32) < a_counts[..., None]
    left = place_blocks(a_values, rows_a, cols_a, live_a)
    row_b = row_ids[..., 0]
    col_b = col_ids[..., 0]
    layer_b = layer_ids[..., 0]
    piece_b = N_ROW * layer_b + (row_b + col_b) % N_ROW
    rows_b = piece_b[..., None] * TILE_INNER + b_places[..., 0]
    cols_b = col_b[..., None] * TILE_COLS + b_places[..., 1]
    live_b = jnp.arange(CAP_B, dtype=jnp.int32) < b_counts[..., None]
    right = place_blocks(b_values, rows_b, cols_b, live_b)
    return jnp.dot(left, right, precision=lax.Precision.HIGHEST, preferred_element_type=jnp.float32)
```

```python
import functools

import jax
import jax.numpy as jnp
from jax import lax
from jax.experimental import pallas as pl
from jax.experimental.pallas import tpu as pltpu
from jax.sharding import PartitionSpec as P

MESH = pl.DeviceIdType.MESH
TILE_ROWS = 8
CHUNKS = 4


def spread(inner, tile_cols, a_pos, a_num, b_pos, b_num, a_val, b_val, a_out, b_out, a_inv, b_inv):
    slots, caps, width = a_val.shape[0], a_val.shape[1], a_val.shape[2]
    for m in range(slots):
        for t in range(TILE_ROWS * inner):
            a_inv[m, t] = -1
        for s in range(caps):
            spot = a_pos[m, 2 * s] * inner + a_pos[m, 2 * s + 1]
            a_inv[m, spot] = jnp.where(s < a_num[m], s, a_inv[m, spot])
    for t in range(inner * tile_cols):
        b_inv[t] = -1
    for s in range(b_val.shape[0]):
        spot = b_pos[2 * s] * tile_cols + b_pos[2 * s + 1]
        b_inv[spot] = jnp.where(s < b_num[0], s, b_inv[spot])

    def block(ref, slot):
        value = ref[jnp.maximum(slot, 0)]
        return jnp.where(slot >= 0, value, jnp.zeros_like(value))

    for m in range(slots):
        for r in range(TILE_ROWS):
            pair = [block(a_val.at[m], a_inv[m, r * inner + c]) for c in range(inner)]
            a_out[pl.ds(r * width, width), pl.ds(m * inner * width, inner * width)] = jnp.concatenate(pair, 1)
    for r in range(inner):
        for c in range(0, tile_cols, 2):
            pair = [block(b_val, b_inv[r * tile_cols + c + d]) for d in range(2)]
            b_out[pl.ds(r * width, width), pl.ds(c * width, 2 * width)] = jnp.concatenate(pair, 1)


def halves(x):
    high = x.astype(jnp.bfloat16)
    return high, (x - high.astype(jnp.float32)).astype(jnp.bfloat16)


def dot(x, y):
    xh, xl = halves(x)
    yh, yl = halves(y)
    f = functools.partial(jnp.dot, preferred_element_type=jnp.float32)
    return f(xh, yh) + (f(xh, yl) + f(xl, yh))


def powers(n):
    out, b = [], n // 2
    while b:
        out.append(b)
        b //= 2
    return out


def multiply(rows, cols, part, depth, n_copies, a_ref, b_ref, out_ref, a_full, b_full, sent, landed, send_sem, recv_sem, local_sem):
    i, j, l = lax.axis_index("row"), lax.axis_index("col"), lax.axis_index("layer")
    row_bits, col_bits = powers(rows), powers(cols)
    slots = rows // cols
    width = b_ref.shape[1] // CHUNKS
    partner = l + 1 - 2 * (l % 2)
    is_inner = jnp.logical_or(l == 1, l == 2)
    is_outer = jnp.logical_or(l == 0, l == 3)
    inner_dest = 1 + l // 2
    outer_dest = 3 * (l // 2)
    far_lo = pl.multiple_of(2 * part * (1 - l // 2), 2 * part)
    near_lo = pl.multiple_of(2 * part * (l // 2), 2 * part)
    inner_lo = pl.multiple_of(part * inner_dest, part)
    outer_lo = pl.multiple_of(part * outer_dest, part)

    def flip(x, bit):
        return x + bit - 2 * bit * ((x // bit) % 2)

    ids = iter(range(n_copies))
    pending = []

    def copy(src, dst, device, back=0):
        k = next(ids)
        return pltpu.make_async_remote_copy(
            src_ref=src, dst_ref=dst, send_sem=send_sem.at[k], recv_sem=recv_sem.at[k - back],
            device_id=device, device_id_type=MESH)

    def when(cond, act):
        if cond is None:
            act()
        else:
            pl.when(cond)(act)

    def start(copies, cond=None):
        when(cond, lambda: [c.start() for c in copies] and None)
        pending.append((copies, cond))

    def arrive(copies, cond=None):
        when(cond, lambda: [c.wait_recv() for c in copies] and None)

    def depart(entry):
        copies, cond = entry
        when(cond, lambda: [c.wait_send() for c in copies] and None)

    def at(piece):
        return pl.ds(pl.multiple_of(piece * depth, depth), depth)

    def b_view(q, piece, c):
        return b_full.at[q, at(piece), pl.ds(c * width, width)]

    def b_stage(q, c, stage):
        bit = row_bits[stage]
        offsets = [0]
        for b in row_bits[:stage]:
            offsets = offsets + [o + b for o in offsets]
        copies = []
        for o in offsets:
            owner = i
            for b in row_bits[:stage]:
                if o & b:
                    owner = flip(owner, b)
            piece = (owner + j) % rows
            if q == 0 and o == 0:
                src = b_ref.at[:, pl.ds(c * width, width)]
            else:
                src = b_view(q, piece, c)
            copies.append(copy(src, b_view(q, piece, c), {"row": flip(i, bit)}))
        return copies

    def a_view(q, lo, size, piece):
        return a_full.at[q, pl.ds(lo, size), at(piece)]

    def a_stage(q, lo, size, stage):
        bit = col_bits[stage]
        owners = [j]
        for b in col_bits[:stage]:
            owners = owners + [flip(o, b) for o in owners]
        copies = []
        for n, o in enumerate(owners):
            for m in range(slots):
                piece = (i + o + cols * m) % rows
                if q == 0 and n == 0:
                    src = a_ref.at[pl.ds(lo, size), pl.ds(m * depth, depth)]
                else:
                    src = a_view(q, lo, size, piece)
                copies.append(copy(src, a_view(q, lo, size, piece), {"col": flip(j, bit)}))
        return copies

    my_pieces = [(i + j + cols * m) % rows for m in range(slots)]
    to_partner = {"layer": partner}

    def z_a(lo, size):
        return [copy(a_ref.at[pl.ds(lo, size), pl.ds(m * depth, depth)],
                     a_view(1, lo, size, my_pieces[m]), to_partner) for m in range(slots)]

    def z_b(c):
        return [copy(b_ref.at[:, pl.ds(c * width, width)], b_view(1, my_pieces[0], c), to_partner)]

    barrier = pltpu.get_barrier_semaphore()
    peers = [{"row": flip(i, b)} for b in row_bits] + [{"col": flip(j, b)} for b in col_bits]
    peers += [{"layer": (l + d) % 4} for d in (1, 2, 3)]
    for peer in peers:
        pl.semaphore_signal(barrier, inc=1, device_id=peer, device_id_type=MESH)
    pl.semaphore_wait(barrier, len(peers))

    def a_finish(q, lo, size, first, cond):
        arrive(first, cond)
        for stage in range(1, len(col_bits)):
            more = a_stage(q, lo, size, stage)
            start(more, cond)
            arrive(more, cond)

    def b_relay(q, c, first, cond):
        arrive(first, cond)
        for stage in range(1, len(row_bits)):
            more = b_stage(q, c, stage)
            start(more, cond)
            if stage < len(row_bits) - 1:
                arrive(more, cond)
        return more

    za_far, zb = z_a(far_lo, 2 * part), [z_b(c) for c in range(CHUNKS)]
    za_inner = z_a(inner_lo, part)
    start(za_far, is_outer)
    far0 = a_stage(0, far_lo, 2 * part, 0)
    start(far0, is_inner)
    b0 = [None] * CHUNKS
    b1 = [None] * CHUNKS
    b0[0] = b_stage(0, 0, 0)
    start(b0[0])
    start(zb[0], is_outer)
    own = [pltpu.make_async_copy(b_ref, b_full.at[0, at(my_pieces[0])], local_sem.at[0])]
    for m in range(slots):
        own.append(pltpu.make_async_copy(
            a_ref.at[:, pl.ds(m * depth, depth)], a_full.at[0, :, at(my_pieces[m])], local_sem.at[1 + m]))
    for c in own:
        c.start()
    near0 = a_stage(0, near_lo, 2 * part, 0)
    start(near0, is_outer)
    last0 = [None] * CHUNKS
    last1 = [None] * CHUNKS
    last0[0] = b_relay(0, 0, b0[0], None)
    b0[1] = b_stage(0, 1, 0)
    arrive(za_far, is_inner)
    far1 = a_stage(1, far_lo, 2 * part, 0)
    start(far1, is_inner)
    arrive(zb[0], is_inner)
    b1[0] = b_stage(1, 0, 0)
    start(b1[0], is_inner)
    start(b0[1])
    depart((za_far, is_outer))
    pending.remove((za_far, is_outer))
    start(zb[1], is_outer)
    last1[0] = b_relay(1, 0, b1[0], is_inner)
    for c in own:
        c.wait()
    a_finish(0, far_lo, 2 * part, far0, is_inner)
    a_finish(1, far_lo, 2 * part, far1, is_inner)
    start(near0, is_inner)

    step = min(rows * depth, 512)

    def product(q, lo, size, c):
        total = rows * depth // step

        def term(k):
            at_k = pl.ds(pl.multiple_of(k * step, step), step)
            return dot(a_full[q, pl.ds(lo, size), at_k], b_full[q, at_k, pl.ds(c * width, width)])

        if total == 1:
            return term(0)
        return lax.fori_loop(0, total, lambda k, s: s + term(k), jnp.zeros((size, width), jnp.float32))

    def chunk(c):
        return pl.ds(c * width, width)

    results = []

    def far_chunk(c):
        def act():
            value = product(0, far_lo, 2 * part, c) + product(1, far_lo, 2 * part, c)
            sent[0, :, chunk(c)] = value[:part]
            sent[1, :, chunk(c)] = value[part:]
        when(is_inner, act)
        first = 2 * (1 - l // 2)
        copies = []
        for n in range(2):
            copies.append(copy(sent.at[n, :, chunk(c)], landed.at[0, :, chunk(c)], {"layer": first + n}, n))
        start(copies, is_inner)
        return copies[0]

    def near_chunk(c):
        def act():
            sent[2, :, chunk(c)] = product(0, outer_lo, part, c)
        when(is_inner, act)
        copies = [copy(sent.at[2, :, chunk(c)], landed.at[1, :, chunk(c)], to_partner)]
        start(copies, is_inner)
        return copies[0]

    def outer_chunk(c):
        def act():
            out_ref[:, chunk(c)] = product(0, outer_lo, part, c)
        when(is_outer, act)

    def inner_chunk(c):
        def act():
            out_ref[:, chunk(c)] = product(0, inner_lo, part, c) + product(1, inner_lo, part, c)
        when(is_inner, act)

    far_sent, near_sent = [None] * CHUNKS, [None] * CHUNKS
    for c in range(CHUNKS):
        if c + 1 < CHUNKS:
            arrive(zb[c + 1], is_inner)
            b1[c + 1] = b_stage(1, c + 1, 0)
            start(b1[c + 1], is_inner)
            if c + 2 < CHUNKS:
                b0[c + 2] = b_stage(0, c + 2, 0)
                start(b0[c + 2])
                start(zb[c + 2], is_outer)
            else:
                start(za_inner, is_outer)
        arrive(last0[c])
        arrive(last1[c], is_inner)
        far_sent[c] = far_chunk(c)
        if c + 1 < CHUNKS:
            last0[c + 1] = b_relay(0, c + 1, b0[c + 1], None)
            last1[c + 1] = b_relay(1, c + 1, b1[c + 1], is_inner)
        if c == 0:
            a_finish(0, near_lo, 2 * part, near0, None)
        else:
            near_sent[c - 1] = near_chunk(c - 1)
        outer_chunk(c)
    near_sent[CHUNKS - 1] = near_chunk(CHUNKS - 1)
    arrive(za_inner, is_inner)
    inner1 = a_stage(1, inner_lo, part, 0)
    start(inner1, is_inner)
    a_finish(1, inner_lo, part, inner1, is_inner)
    for c in range(CHUNKS):
        inner_chunk(c)
        far_sent[c].wait_recv()
        out_ref[:, chunk(c)] += landed[0, :, chunk(c)]

        def add(c=c):
            near_sent[c].wait_recv()
            out_ref[:, chunk(c)] += landed[1, :, chunk(c)]
        when(is_outer, add)
    for entry in pending:
        depart(entry)


def body(rows, cols, a_values, a_places, a_counts, b_values, b_places, b_counts):
    a_vals = a_values.reshape(a_values.shape[3:])
    b_vals = b_values.reshape(b_values.shape[3:])
    slots, cap, width = a_vals.shape[:3]
    layers = lax.axis_size("layer")
    inner = TILE_ROWS // layers
    tile_cols = TILE_ROWS * rows // cols
    a_pos = a_places.reshape(slots, 2 * cap)
    a_num = a_counts.reshape(slots)
    b_pos = b_places.reshape(2 * b_vals.shape[0])
    b_num = b_counts.reshape(1)
    depth, part = inner * width, TILE_ROWS * width // layers
    full_rows, full_cols = TILE_ROWS * width, tile_cols * width
    f32 = jnp.float32
    vmem = pl.BlockSpec(memory_space=pltpu.VMEM)
    smem = pl.BlockSpec(memory_space=pltpu.SMEM)
    a_dense, b_dense = pl.pallas_call(
        functools.partial(spread, inner, tile_cols),
        out_shape=(jax.ShapeDtypeStruct((full_rows, slots * depth), f32), jax.ShapeDtypeStruct((depth, full_cols), f32)),
        in_specs=[smem] * 4 + [vmem] * 2,
        out_specs=(vmem, vmem),
        scratch_shapes=[pltpu.SMEM((slots, TILE_ROWS * inner), jnp.int32), pltpu.SMEM((inner * tile_cols,), jnp.int32)],
    )(a_pos, a_num, b_pos, b_num, a_vals, b_vals)

    n_copies = 2 * CHUNKS * (rows - 1) + 4 * slots * (cols - 1) + 2 * slots + CHUNKS * 4
    return pl.pallas_call(
        functools.partial(multiply, rows, cols, part, depth, n_copies),
        out_shape=jax.ShapeDtypeStruct((part, full_cols), f32),
        in_specs=[vmem, vmem],
        out_specs=vmem,
        scratch_shapes=[
            pltpu.VMEM((2, full_rows, rows * depth), f32),
            pltpu.VMEM((2, rows * depth, full_cols), f32),
            pltpu.VMEM((3, part, full_cols), f32),
            pltpu.VMEM((2, part, full_cols), f32),
            pltpu.SemaphoreType.DMA((n_copies,)),
            pltpu.SemaphoreType.DMA((n_copies,)),
            pltpu.SemaphoreType.DMA((1 + slots,)),
        ],
        compiler_params=pltpu.CompilerParams(collective_id=0, has_side_effects=True, vmem_limit_bytes=48 * 2**20),
    )(a_dense, b_dense)


def solution(mesh):
    in_specs = (
        P("row", "col", "layer", None, None, None, None),
        P("row", "col", "layer", None, None, None),
        P("row", "col", "layer", None),
        P("row", "col", "layer", None, None, None),
        P("row", "col", "layer", None, None),
        P("row", "col", "layer"),
    )
    out_specs = P(("row", "layer"), "col")
    call = functools.partial(body, mesh.shape["row"], mesh.shape["col"])
    return jax.shard_map(call, mesh=mesh, in_specs=in_specs, out_specs=out_specs, check_vma=False)
```

```python
import functools

import jax
import jax.numpy as jnp
from jax import lax
from jax.experimental import pallas as pl
from jax.experimental.pallas import tpu as pltpu
from jax.sharding import PartitionSpec as P

MESH = pl.DeviceIdType.MESH
TILE_ROWS = 8
CHUNKS = 4


def inverse(spots, total, bits):
    each = 32 // bits
    words = [jnp.int32(0)] * (-(-total // each))
    for s, spot in enumerate(spots):
        mark = jnp.left_shift(jnp.int32(s + 1), bits * (spot % each))
        for w in range(len(words)):
            inside = jnp.logical_and(spot >= w * each, spot < (w + 1) * each)
            words[w] = words[w] + jnp.where(inside, mark, 0)
    return [jnp.right_shift(words[t // each], bits * (t % each)) & (2**bits - 1) for t in range(total)]


def halves(x):
    high = x.astype(jnp.bfloat16)
    return high, (x - high.astype(jnp.float32)).astype(jnp.bfloat16)


def dot(x, y):
    xh, xl = halves(x)
    yh, yl = halves(y)
    f = functools.partial(jnp.dot, preferred_element_type=jnp.float32)
    return f(xh, yh) + (f(xh, yl) + f(xl, yh))


def powers(n):
    out, b = [], n // 2
    while b:
        out.append(b)
        b //= 2
    return out


def multiply(rows, cols, part, depth, n_copies, *refs):
    hbm, out_ref, held = refs[:6], refs[6], refs[7:13]
    a_pos, a_num, b_pos, b_num, a_val, b_val = held
    a_full, b_full, sent, landed, send_sem, recv_sem, local_sem = refs[13:]
    i, j, l = lax.axis_index("row"), lax.axis_index("col"), lax.axis_index("layer")
    row_bits, col_bits = powers(rows), powers(cols)
    slots = rows // cols
    width = b_full.shape[2] // CHUNKS
    partner = l + 1 - 2 * (l % 2)
    is_inner = jnp.logical_or(l == 1, l == 2)
    is_outer = jnp.logical_or(l == 0, l == 3)
    inner_dest = 1 + l // 2
    outer_dest = 3 * (l // 2)
    far_lo = pl.multiple_of(2 * part * (1 - l // 2), 2 * part)
    near_lo = pl.multiple_of(2 * part * (l // 2), 2 * part)
    inner_lo = pl.multiple_of(part * inner_dest, part)
    outer_lo = pl.multiple_of(part * outer_dest, part)

    def flip(x, bit):
        return x + bit - 2 * bit * ((x // bit) % 2)

    ids = iter(range(n_copies))
    pending = []

    def copy(src, dst, device, back=0):
        k = next(ids)
        return pltpu.make_async_remote_copy(
            src_ref=src, dst_ref=dst, send_sem=send_sem.at[k], recv_sem=recv_sem.at[k - back],
            device_id=device, device_id_type=MESH)

    def when(cond, act):
        if cond is None:
            act()
        else:
            pl.when(cond)(act)

    def start(copies, cond=None):
        when(cond, lambda: [c.start() for c in copies] and None)
        pending.append((copies, cond))

    def arrive(copies, cond=None):
        when(cond, lambda: [c.wait_recv() for c in copies] and None)

    def depart(entry):
        copies, cond = entry
        when(cond, lambda: [c.wait_send() for c in copies] and None)

    def at(piece):
        return pl.ds(pl.multiple_of(piece * depth, depth), depth)

    def b_view(q, piece, c):
        return b_full.at[q, at(piece), pl.ds(c * width, width)]

    def b_stage(q, c, stage):
        bit = row_bits[stage]
        offsets = [0]
        for b in row_bits[:stage]:
            offsets = offsets + [o + b for o in offsets]
        copies = []
        for o in offsets:
            owner = i
            for b in row_bits[:stage]:
                if o & b:
                    owner = flip(owner, b)
            piece = (owner + j) % rows
            src = b_view(q, piece, c)
            copies.append(copy(src, b_view(q, piece, c), {"row": flip(i, bit)}))
        return copies

    def a_view(q, lo, size, piece):
        return a_full.at[q, pl.ds(lo, size), at(piece)]

    def a_stage(q, lo, size, stage):
        bit = col_bits[stage]
        owners = [j]
        for b in col_bits[:stage]:
            owners = owners + [flip(o, b) for o in owners]
        copies = []
        for o in owners:
            for m in range(slots):
                piece = (i + o + cols * m) % rows
                src = a_view(q, lo, size, piece)
                copies.append(copy(src, a_view(q, lo, size, piece), {"col": flip(j, bit)}))
        return copies

    my_pieces = [(i + j + cols * m) % rows for m in range(slots)]
    to_partner = {"layer": partner}

    def z_a(lo, size):
        return [copy(a_view(0, lo, size, my_pieces[m]),
                     a_view(1, lo, size, my_pieces[m]), to_partner) for m in range(slots)]

    def z_b(c):
        return [copy(b_view(0, my_pieces[0], c), b_view(1, my_pieces[0], c), to_partner)]

    loads = [pltpu.make_async_copy(src, dst, local_sem.at[n]) for n, (src, dst) in enumerate(zip(hbm, held))]
    for load in loads:
        load.start()

    barrier = pltpu.get_barrier_semaphore()
    peers = [{"row": flip(i, b)} for b in row_bits] + [{"col": flip(j, b)} for b in col_bits]
    peers += [{"layer": (l + d) % 4} for d in (1, 2, 3)]
    for peer in peers:
        pl.semaphore_signal(barrier, inc=1, device_id=peer, device_id_type=MESH)

    for load in loads[:4]:
        load.wait()

    block = a_val.shape[-1]
    inner, tile_cols = depth // block, b_full.shape[2] // block
    caps = a_val.shape[1]
    a_slot = [
        inverse([jnp.where(s < a_num[m], a_pos[m, 0, s] * inner + a_pos[m, 1, s], -1) for s in range(caps)],
                TILE_ROWS * inner, 4)
        for m in range(slots)
    ]
    b_slot = inverse(
        [jnp.where(s < b_num[0], b_pos[0, s] * tile_cols + b_pos[1, s], -1) for s in range(b_val.shape[0])],
        inner * tile_cols, 8)

    def stored(ref, slot):
        value = ref[jnp.maximum(slot - 1, 0)]
        return jnp.where(slot > 0, value, jnp.zeros_like(value))

    def a_dense():
        for m in range(slots):
            for r in range(TILE_ROWS):
                parts = [stored(a_val.at[m], a_slot[m][r * inner + k]) for k in range(inner)]
                a_full[0, pl.ds(r * block, block), at(my_pieces[m])] = jnp.concatenate(parts, 1)

    def b_dense(c):
        for r in range(inner):
            rows_r = pl.ds(pl.multiple_of(my_pieces[0] * depth + r * block, block), block)
            for k in range(c * width // block, (c + 1) * width // block, 2):
                parts = [stored(b_val, b_slot[r * tile_cols + k + d]) for d in range(2)]
                b_full[0, rows_r, pl.ds(k * block, 2 * block)] = jnp.concatenate(parts, 1)

    for load in loads[4:]:
        load.wait()
    a_dense()
    b_dense(0)
    pl.semaphore_wait(barrier, len(peers))

    def a_finish(q, lo, size, first, cond):
        arrive(first, cond)
        for stage in range(1, len(col_bits)):
            more = a_stage(q, lo, size, stage)
            start(more, cond)
            arrive(more, cond)

    def b_relay(q, c, first, cond):
        arrive(first, cond)
        for stage in range(1, len(row_bits)):
            more = b_stage(q, c, stage)
            start(more, cond)
            if stage < len(row_bits) - 1:
                arrive(more, cond)
        return more

    za_far, zb = z_a(far_lo, 2 * part), [z_b(c) for c in range(CHUNKS)]
    za_inner = z_a(inner_lo, part)
    start(za_far, is_outer)
    far0 = a_stage(0, far_lo, 2 * part, 0)
    start(far0, is_inner)
    b0 = [None] * CHUNKS
    b1 = [None] * CHUNKS
    b0[0] = b_stage(0, 0, 0)
    start(b0[0])
    start(zb[0], is_outer)
    for c in range(1, CHUNKS):
        b_dense(c)
    near0 = a_stage(0, near_lo, 2 * part, 0)
    start(near0, is_outer)
    last0 = [None] * CHUNKS
    last1 = [None] * CHUNKS
    last0[0] = b_relay(0, 0, b0[0], None)
    b0[1] = b_stage(0, 1, 0)
    arrive(za_far, is_inner)
    far1 = a_stage(1, far_lo, 2 * part, 0)
    start(far1, is_inner)
    arrive(zb[0], is_inner)
    b1[0] = b_stage(1, 0, 0)
    start(b1[0], is_inner)
    start(b0[1])
    depart((za_far, is_outer))
    pending.remove((za_far, is_outer))
    start(zb[1], is_outer)
    last1[0] = b_relay(1, 0, b1[0], is_inner)
    a_finish(0, far_lo, 2 * part, far0, is_inner)
    a_finish(1, far_lo, 2 * part, far1, is_inner)
    start(near0, is_inner)

    step = min(rows * depth, 512)

    def product(q, lo, size, c):
        total = rows * depth // step

        def term(k):
            at_k = pl.ds(pl.multiple_of(k * step, step), step)
            return dot(a_full[q, pl.ds(lo, size), at_k], b_full[q, at_k, pl.ds(c * width, width)])

        if total == 1:
            return term(0)
        return lax.fori_loop(0, total, lambda k, s: s + term(k), jnp.zeros((size, width), jnp.float32))

    def chunk(c):
        return pl.ds(c * width, width)

    results = []

    def far_chunk(c):
        def act():
            value = product(0, far_lo, 2 * part, c) + product(1, far_lo, 2 * part, c)
            sent[0, :, chunk(c)] = value[:part]
            sent[1, :, chunk(c)] = value[part:]
        when(is_inner, act)
        first = 2 * (1 - l // 2)
        copies = []
        for n in range(2):
            copies.append(copy(sent.at[n, :, chunk(c)], landed.at[0, :, chunk(c)], {"layer": first + n}, n))
        start(copies, is_inner)
        return copies[0]

    def near_chunk(c):
        def act():
            sent[2, :, chunk(c)] = product(0, outer_lo, part, c)
        when(is_inner, act)
        copies = [copy(sent.at[2, :, chunk(c)], landed.at[1, :, chunk(c)], to_partner)]
        start(copies, is_inner)
        return copies[0]

    def outer_chunk(c):
        def act():
            out_ref[:, chunk(c)] = product(0, outer_lo, part, c)
        when(is_outer, act)

    def inner_chunk(c):
        def act():
            out_ref[:, chunk(c)] = product(0, inner_lo, part, c) + product(1, inner_lo, part, c)
        when(is_inner, act)

    far_sent, near_sent = [None] * CHUNKS, [None] * CHUNKS
    for c in range(CHUNKS):
        if c + 1 < CHUNKS:
            arrive(zb[c + 1], is_inner)
            b1[c + 1] = b_stage(1, c + 1, 0)
            start(b1[c + 1], is_inner)
            if c + 2 < CHUNKS:
                b0[c + 2] = b_stage(0, c + 2, 0)
                start(b0[c + 2])
                start(zb[c + 2], is_outer)
            else:
                start(za_inner, is_outer)
        arrive(last0[c])
        arrive(last1[c], is_inner)
        far_sent[c] = far_chunk(c)
        if c + 1 < CHUNKS:
            last0[c + 1] = b_relay(0, c + 1, b0[c + 1], None)
            last1[c + 1] = b_relay(1, c + 1, b1[c + 1], is_inner)
        if c == 0:
            a_finish(0, near_lo, 2 * part, near0, None)
        else:
            near_sent[c - 1] = near_chunk(c - 1)
        outer_chunk(c)
    near_sent[CHUNKS - 1] = near_chunk(CHUNKS - 1)
    arrive(za_inner, is_inner)
    inner1 = a_stage(1, inner_lo, part, 0)
    start(inner1, is_inner)
    a_finish(1, inner_lo, part, inner1, is_inner)
    for c in range(CHUNKS):
        inner_chunk(c)
        far_sent[c].wait_recv()
        out_ref[:, chunk(c)] += landed[0, :, chunk(c)]

        def add(c=c):
            near_sent[c].wait_recv()
            out_ref[:, chunk(c)] += landed[1, :, chunk(c)]
        when(is_outer, add)
    for entry in pending:
        depart(entry)


def body(rows, cols, a_values, a_places, a_counts, b_values, b_places, b_counts):
    a_vals = a_values.reshape(a_values.shape[3:])
    b_vals = b_values.reshape(b_values.shape[3:])
    slots, width = a_vals.shape[0], a_vals.shape[2]
    layers = lax.axis_size("layer")
    inner = TILE_ROWS // layers
    tile_cols = TILE_ROWS * rows // cols
    a_pos = jnp.swapaxes(a_places.reshape(a_places.shape[3:]), 1, 2)
    a_num = a_counts.reshape(slots)
    b_pos = b_places.reshape(b_places.shape[3:]).T
    b_num = b_counts.reshape(1)
    depth, part = inner * width, TILE_ROWS * width // layers
    full_rows, full_cols = TILE_ROWS * width, tile_cols * width
    f32 = jnp.float32
    vmem = pl.BlockSpec(memory_space=pltpu.VMEM)
    n_copies = 2 * CHUNKS * (rows - 1) + 4 * slots * (cols - 1) + 2 * slots + CHUNKS * 4
    return pl.pallas_call(
        functools.partial(multiply, rows, cols, part, depth, n_copies),
        out_shape=jax.ShapeDtypeStruct((part, full_cols), f32),
        in_specs=[pl.BlockSpec(memory_space=pltpu.HBM)] * 6,
        out_specs=vmem,
        scratch_shapes=[
            *[pltpu.SMEM(x.shape, jnp.int32) for x in (a_pos, a_num, b_pos, b_num)],
            pltpu.VMEM(a_vals.shape, f32),
            pltpu.VMEM(b_vals.shape, f32),
            pltpu.VMEM((2, full_rows, rows * depth), f32),
            pltpu.VMEM((2, rows * depth, full_cols), f32),
            pltpu.VMEM((3, part, full_cols), f32),
            pltpu.VMEM((2, part, full_cols), f32),
            pltpu.SemaphoreType.DMA((n_copies,)),
            pltpu.SemaphoreType.DMA((n_copies,)),
            pltpu.SemaphoreType.DMA((6,)),
        ],
        compiler_params=pltpu.CompilerParams(collective_id=0, has_side_effects=True, vmem_limit_bytes=63 * 2**20),
    )(a_pos, a_num, b_pos, b_num, a_vals, b_vals)


def solution(mesh):
    in_specs = (
        P("row", "col", "layer", None, None, None, None),
        P("row", "col", "layer", None, None, None),
        P("row", "col", "layer", None),
        P("row", "col", "layer", None, None, None),
        P("row", "col", "layer", None, None),
        P("row", "col", "layer"),
    )
    out_specs = P(("row", "layer"), "col")
    call = functools.partial(body, mesh.shape["row"], mesh.shape["col"])
    return jax.shard_map(call, mesh=mesh, in_specs=in_specs, out_specs=out_specs, check_vma=False)
```

```python
import functools

import jax
import jax.numpy as jnp
from jax import lax
from jax.experimental import pallas as pl
from jax.experimental.pallas import tpu as pltpu
from jax.sharding import PartitionSpec as P

MESH = pl.DeviceIdType.MESH
TILE_ROWS = 8
CHUNKS = 4


def inverse(spots, total, bits):
    each = 32 // bits
    words = [jnp.int32(0)] * (-(-total // each))
    for s, spot in enumerate(spots):
        mark = jnp.left_shift(jnp.int32(s + 1), bits * (spot % each))
        for w in range(len(words)):
            inside = jnp.logical_and(spot >= w * each, spot < (w + 1) * each)
            words[w] = words[w] + jnp.where(inside, mark, 0)
    return [jnp.right_shift(words[t // each], bits * (t % each)) & (2**bits - 1) for t in range(total)]


def halves(x):
    high = x.astype(jnp.bfloat16)
    return high, (x - high.astype(jnp.float32)).astype(jnp.bfloat16)


def powers(n):
    out, b = [], n // 2
    while b:
        out.append(b)
        b //= 2
    return out


def multiply(rows, cols, part, depth, n_copies, *refs):
    hbm, out_ref, held = refs[:6], refs[6], refs[7:13]
    a_pos, a_num, b_pos, b_num, a_val, b_val = held
    a_full, b_full, a_half, b_half, sent, landed, send_sem, recv_sem, local_sem = refs[13:]
    i, j, l = lax.axis_index("row"), lax.axis_index("col"), lax.axis_index("layer")
    row_bits, col_bits = powers(rows), powers(cols)
    slots = rows // cols
    width = b_full.shape[2] // CHUNKS
    partner = l + 1 - 2 * (l % 2)
    is_inner = jnp.logical_or(l == 1, l == 2)
    is_outer = jnp.logical_or(l == 0, l == 3)
    inner_dest = 1 + l // 2
    outer_dest = 3 * (l // 2)
    dests = [3 - 3 * (l // 2), 2 - l // 2, outer_dest, inner_dest]
    starts = [pl.multiple_of(part * dest, part) for dest in dests]
    near_lo = pl.multiple_of(2 * part * (l // 2), 2 * part)

    def flip(x, bit):
        return x + bit - 2 * bit * ((x // bit) % 2)

    ids = iter(range(n_copies))
    pending = []

    def copy(src, dst, device, back=0):
        k = next(ids)
        return pltpu.make_async_remote_copy(
            src_ref=src, dst_ref=dst, send_sem=send_sem.at[k], recv_sem=recv_sem.at[k - back],
            device_id=device, device_id_type=MESH)

    def when(cond, act):
        if cond is None:
            act()
        else:
            pl.when(cond)(act)

    def start(copies, cond=None):
        when(cond, lambda: [c.start() for c in copies] and None)
        pending.append((copies, cond))

    def arrive(copies, cond=None):
        when(cond, lambda: [c.wait_recv() for c in copies] and None)

    def depart(copies, cond):
        pending[:] = [p for p in pending if p[0] is not copies or p[1] is not cond]
        when(cond, lambda: [c.wait_send() for c in copies] and None)

    def at(piece):
        return pl.ds(pl.multiple_of(piece * depth, depth), depth)

    def b_view(q, piece, c):
        return b_full.at[q, at(piece), pl.ds(c * width, width)]

    def b_stage(q, c, stage):
        bit = row_bits[stage]
        offsets = [0]
        for b in row_bits[:stage]:
            offsets = offsets + [o + b for o in offsets]
        copies = []
        for o in offsets:
            owner = i
            for b in row_bits[:stage]:
                if o & b:
                    owner = flip(owner, b)
            piece = (owner + j) % rows
            src = b_view(q, piece, c)
            copies.append(copy(src, b_view(q, piece, c), {"row": flip(i, bit)}))
        return copies

    def a_view(q, lo, size, piece):
        return a_full.at[q, pl.ds(lo, size), at(piece)]

    def a_stage(q, lo, size, stage):
        bit = col_bits[stage]
        owners = [j]
        for b in col_bits[:stage]:
            owners = owners + [flip(o, b) for o in owners]
        copies = []
        for o in owners:
            for m in range(slots):
                piece = (i + o + cols * m) % rows
                src = a_view(q, lo, size, piece)
                copies.append(copy(src, a_view(q, lo, size, piece), {"col": flip(j, bit)}))
        return copies

    my_pieces = [(i + j + cols * m) % rows for m in range(slots)]
    to_partner = {"layer": partner}

    def z_a(lo, size):
        return [copy(a_view(0, lo, size, my_pieces[m]),
                     a_view(1, lo, size, my_pieces[m]), to_partner) for m in range(slots)]

    def z_b(c):
        return [copy(b_view(0, my_pieces[0], c), b_view(1, my_pieces[0], c), to_partner)]

    loads = [pltpu.make_async_copy(src, dst, local_sem.at[n]) for n, (src, dst) in enumerate(zip(hbm, held))]
    for load in loads:
        load.start()

    barrier = pltpu.get_barrier_semaphore()
    peers = [{"row": flip(i, b)} for b in row_bits] + [{"col": flip(j, b)} for b in col_bits]
    peers += [{"layer": (l + d) % 4} for d in (1, 2, 3)]
    for peer in peers:
        pl.semaphore_signal(barrier, inc=1, device_id=peer, device_id_type=MESH)

    for load in loads[:4]:
        load.wait()

    block = a_val.shape[-1]
    inner, tile_cols = depth // block, b_full.shape[2] // block
    caps = a_val.shape[1]
    a_slot = [
        inverse([jnp.where(s < a_num[m], a_pos[m, 0, s] * inner + a_pos[m, 1, s], -1) for s in range(caps)],
                TILE_ROWS * inner, 4)
        for m in range(slots)
    ]
    b_slot = inverse(
        [jnp.where(s < b_num[0], b_pos[0, s] * tile_cols + b_pos[1, s], -1) for s in range(b_val.shape[0])],
        inner * tile_cols, 8)

    def stored(ref, slot):
        value = ref[jnp.maximum(slot - 1, 0)]
        return jnp.where(slot > 0, value, jnp.zeros_like(value))

    def a_dense():
        for m in range(slots):
            for r in range(TILE_ROWS):
                parts = [stored(a_val.at[m], a_slot[m][r * inner + k]) for k in range(inner)]
                a_full[0, pl.ds(r * block, block), at(my_pieces[m])] = jnp.concatenate(parts, 1)

    def b_dense(c):
        for r in range(inner):
            rows_r = pl.ds(pl.multiple_of(my_pieces[0] * depth + r * block, block), block)
            for k in range(c * width // block, (c + 1) * width // block, 2):
                parts = [stored(b_val, b_slot[r * tile_cols + k + d]) for d in range(2)]
                b_full[0, rows_r, pl.ds(k * block, 2 * block)] = jnp.concatenate(parts, 1)

    for load in loads[4:]:
        load.wait()
    a_dense()
    b_dense(0)
    b_dense(1)
    pl.semaphore_wait(barrier, len(peers))

    def a_finish(q, lo, size, first, cond):
        arrive(first, cond)
        for stage in range(1, len(col_bits)):
            more = a_stage(q, lo, size, stage)
            start(more, cond)
            arrive(more, cond)

    def b_relay(q, c, first, cond):
        arrive(first, cond)
        for stage in range(1, len(row_bits)):
            more = b_stage(q, c, stage)
            start(more, cond)
            if stage < len(row_bits) - 1:
                arrive(more, cond)
        return more

    step = min(rows * depth, 512)

    def steps(act):
        total = rows * depth // step
        if total == 1:
            act(pl.ds(0, step))
        else:
            pl.loop(0, total)(lambda k: act(pl.ds(pl.multiple_of(k * step, step), step)))

    def chunk(c):
        return pl.ds(c * width, width)

    def halve_a(q, n):
        def act(k):
            high, low = halves(a_full[q, pl.ds(starts[n], part), k])
            a_half[q, n, pl.ds(0, part), k] = high
            a_half[q, n, pl.ds(part, part), k] = low
        steps(act)

    def halve_b(q, c):
        def act(k):
            b_half[q, 0, k, chunk(c)], b_half[q, 1, k, chunk(c)] = halves(b_full[q, k, chunk(c)])
        steps(act)

    def product(layers, n, c, out):
        def term(q, k):
            first = jnp.dot(a_half[q, n, :, k], b_half[q, 0, k, chunk(c)], preferred_element_type=jnp.float32)
            other = jnp.dot(a_half[q, n, pl.ds(0, part), k], b_half[q, 1, k, chunk(c)], preferred_element_type=jnp.float32)
            return first[:part] + (first[part:] + other)

        if rows * depth == step:
            value = term(layers[0], pl.ds(0, step))
            for q in layers[1:]:
                value = value + term(q, pl.ds(0, step))
            out[:, chunk(c)] = value
        else:
            out[:, chunk(c)] = jnp.zeros((part, width), jnp.float32)
            for q in layers:
                def act(k, q=q):
                    out[:, chunk(c)] += term(q, k)
                steps(act)

    far_sent, near_sent = [], []
    for c in range(CHUNKS):
        far_sent.append([copy(sent.at[n, :, chunk(c)], landed.at[0, :, chunk(c)], {"layer": dests[n]}, n) for n in range(2)])
        near_sent.append([copy(sent.at[2, :, chunk(c)], landed.at[1, :, chunk(c)], to_partner)])

    def far_chunk(n, c):
        when(is_inner, lambda: product((0, 1), n, c, sent.at[n]))
        start([far_sent[c][n]], is_inner)

    def near_chunk(c):
        when(is_inner, lambda: product((0,), 2, c, sent.at[2]))
        start(near_sent[c], is_inner)

    def chunk_here(c):
        arrive(last0[c])
        arrive(last1[c], is_inner)
        halve_b(0, c)
        when(is_inner, lambda: halve_b(1, c))

    def outer_chunk(c):
        when(is_outer, lambda: product((0,), 2, c, out_ref))

    za = [z_a(starts[n], part) for n in (0, 1, 3)]
    zb = [z_b(c) for c in range(CHUNKS)]
    fo0, fi0 = a_stage(0, starts[0], part, 0), a_stage(0, starts[1], part, 0)
    fo1, fi1 = a_stage(1, starts[0], part, 0), a_stage(1, starts[1], part, 0)
    near0, inner1 = a_stage(0, near_lo, 2 * part, 0), a_stage(1, starts[3], part, 0)
    b0 = [b_stage(0, c, 0) for c in range(CHUNKS)]
    b1 = [b_stage(1, c, 0) for c in range(CHUNKS)]
    last0, last1 = [None] * CHUNKS, [None] * CHUNKS

    start(za[0], is_outer)
    start(fo0, is_inner)
    start(b0[0])
    start(zb[0], is_outer)
    start(near0, is_outer)
    start(b0[1])
    for c in range(2, CHUNKS):
        b_dense(c)
    last0[0] = b_relay(0, 0, b0[0], None)
    arrive(za[0], is_inner)
    start(fo1, is_inner)
    start(fi0, is_inner)
    depart(za[0], is_outer)
    start(za[1], is_outer)
    arrive(zb[0], is_inner)
    start(b1[0], is_inner)
    depart(zb[0], is_outer)
    start(zb[1], is_outer)
    last0[1] = b_relay(0, 1, b0[1], None)
    start(b0[2])
    a_finish(0, starts[0], part, fo0, is_inner)
    a_finish(1, starts[0], part, fo1, is_inner)
    when(is_inner, lambda: [halve_a(q, 0) for q in range(2)] and None)
    last1[0] = b_relay(1, 0, b1[0], is_inner)
    arrive(za[1], is_inner)
    start(fi1, is_inner)
    start(near0, is_inner)
    depart(za[1], is_outer)
    start(zb[2], is_outer)
    chunk_here(0)
    far_chunk(0, 0)
    arrive(zb[1], is_inner)
    start(b1[1], is_inner)
    depart(zb[1], is_outer)
    start(zb[3], is_outer)
    a_finish(0, starts[1], part, fi0, is_inner)
    a_finish(1, starts[1], part, fi1, is_inner)
    when(is_inner, lambda: [halve_a(q, 1) for q in range(2)] and None)
    far_chunk(1, 0)
    last0[2] = b_relay(0, 2, b0[2], None)
    start(b0[3])
    arrive(zb[2], is_inner)
    start(b1[2], is_inner)
    depart(zb[2], is_outer)
    start(za[2], is_outer)
    last1[1] = b_relay(1, 1, b1[1], is_inner)
    chunk_here(1)
    far_chunk(0, 1)
    far_chunk(1, 1)
    arrive(zb[3], is_inner)
    start(b1[3], is_inner)
    a_finish(0, near_lo, 2 * part, near0, None)
    halve_a(0, 2)
    when(is_inner, lambda: halve_a(0, 3))
    near_chunk(0)
    outer_chunk(0)
    outer_chunk(1)
    last0[3] = b_relay(0, 3, b0[3], None)
    last1[2] = b_relay(1, 2, b1[2], is_inner)
    chunk_here(2)
    far_chunk(0, 2)
    far_chunk(1, 2)
    near_chunk(1)
    outer_chunk(2)
    arrive(za[2], is_inner)
    start(inner1, is_inner)
    last1[3] = b_relay(1, 3, b1[3], is_inner)
    chunk_here(3)
    far_chunk(0, 3)
    far_chunk(1, 3)
    near_chunk(2)
    near_chunk(3)
    outer_chunk(3)
    a_finish(1, starts[3], part, inner1, is_inner)
    when(is_inner, lambda: halve_a(1, 3))
    for c in range(CHUNKS):
        when(is_inner, lambda c=c: product((0, 1), 3, c, out_ref))
    for c in range(CHUNKS):
        far_sent[c][0].wait_recv()
        out_ref[:, chunk(c)] += landed[0, :, chunk(c)]

        def add(c=c):
            near_sent[c][0].wait_recv()
            out_ref[:, chunk(c)] += landed[1, :, chunk(c)]
        when(is_outer, add)
    for copies, cond in list(pending):
        depart(copies, cond)


def body(rows, cols, a_values, a_places, a_counts, b_values, b_places, b_counts):
    a_vals = a_values.reshape(a_values.shape[3:])
    b_vals = b_values.reshape(b_values.shape[3:])
    slots, width = a_vals.shape[0], a_vals.shape[2]
    layers = lax.axis_size("layer")
    inner = TILE_ROWS // layers
    tile_cols = TILE_ROWS * rows // cols
    a_pos = jnp.swapaxes(a_places.reshape(a_places.shape[3:]), 1, 2)
    a_num = a_counts.reshape(slots)
    b_pos = b_places.reshape(b_places.shape[3:]).T
    b_num = b_counts.reshape(1)
    depth, part = inner * width, TILE_ROWS * width // layers
    full_rows, full_cols = TILE_ROWS * width, tile_cols * width
    f32 = jnp.float32
    vmem = pl.BlockSpec(memory_space=pltpu.VMEM)
    n_copies = 2 * CHUNKS * (rows - 1) + 6 * slots * (cols - 1) + 3 * slots + 4 * CHUNKS
    return pl.pallas_call(
        functools.partial(multiply, rows, cols, part, depth, n_copies),
        out_shape=jax.ShapeDtypeStruct((part, full_cols), f32),
        in_specs=[pl.BlockSpec(memory_space=pltpu.HBM)] * 6,
        out_specs=vmem,
        scratch_shapes=[
            *[pltpu.SMEM(x.shape, jnp.int32) for x in (a_pos, a_num, b_pos, b_num)],
            pltpu.VMEM(a_vals.shape, f32),
            pltpu.VMEM(b_vals.shape, f32),
            pltpu.VMEM((2, full_rows, rows * depth), f32),
            pltpu.VMEM((2, rows * depth, full_cols), f32),
            pltpu.VMEM((2, layers, 2 * part, rows * depth), jnp.bfloat16),
            pltpu.VMEM((2, 2, rows * depth, full_cols), jnp.bfloat16),
            pltpu.VMEM((3, part, full_cols), f32),
            pltpu.VMEM((2, part, full_cols), f32),
            pltpu.SemaphoreType.DMA((n_copies,)),
            pltpu.SemaphoreType.DMA((n_copies,)),
            pltpu.SemaphoreType.DMA((6,)),
        ],
        compiler_params=pltpu.CompilerParams(collective_id=0, has_side_effects=True, vmem_limit_bytes=63 * 2**20),
    )(a_pos, a_num, b_pos, b_num, a_vals, b_vals)


def solution(mesh):
    in_specs = (
        P("row", "col", "layer", None, None, None, None),
        P("row", "col", "layer", None, None, None),
        P("row", "col", "layer", None),
        P("row", "col", "layer", None, None, None),
        P("row", "col", "layer", None, None),
        P("row", "col", "layer"),
    )
    out_specs = P(("row", "layer"), "col")
    call = functools.partial(body, mesh.shape["row"], mesh.shape["col"])
    return jax.shard_map(call, mesh=mesh, in_specs=in_specs, out_specs=out_specs, check_vma=False)
```

```python
import functools

import jax
import jax.numpy as jnp
from jax import lax
from jax.experimental import pallas as pl
from jax.experimental.pallas import tpu as pltpu
from jax.sharding import PartitionSpec as P

MESH = pl.DeviceIdType.MESH
TILE_ROWS = 8
CHUNKS = 4


def inverse(spots, total, bits):
    each = 32 // bits
    words = [jnp.int32(0)] * (-(-total // each))
    for s, spot in enumerate(spots):
        mark = jnp.left_shift(jnp.int32(s + 1), bits * (spot % each))
        for w in range(len(words)):
            inside = jnp.logical_and(spot >= w * each, spot < (w + 1) * each)
            words[w] = words[w] + jnp.where(inside, mark, 0)
    return [jnp.right_shift(words[t // each], bits * (t % each)) & (2**bits - 1) for t in range(total)]


def halves(x):
    high = x.astype(jnp.bfloat16)
    return high, (x - high.astype(jnp.float32)).astype(jnp.bfloat16)


def powers(n):
    out, b = [], n // 2
    while b:
        out.append(b)
        b //= 2
    return out


def multiply(rows, cols, part, depth, n_copies, *refs):
    hbm, out_ref, held = refs[:6], refs[6], refs[7:13]
    a_pos, a_num, b_pos, b_num, a_val, b_val = held
    a_full, b_full, a_half, b_half, sent, landed, send_sem, recv_sem, local_sem = refs[13:]
    i, j, l = lax.axis_index("row"), lax.axis_index("col"), lax.axis_index("layer")
    row_bits, col_bits = powers(rows), powers(cols)
    slots = rows // cols
    width = b_full.shape[3]
    partner = l + 1 - 2 * (l % 2)
    is_inner = jnp.logical_or(l == 1, l == 2)
    is_outer = jnp.logical_or(l == 0, l == 3)
    inner_dest = 1 + l // 2
    outer_dest = 3 * (l // 2)
    dests = [3 - 3 * (l // 2), 2 - l // 2, outer_dest, inner_dest]
    starts = [pl.multiple_of(part * dest, part) for dest in dests]
    near_lo = pl.multiple_of(2 * part * (l // 2), 2 * part)

    def flip(x, bit):
        return x + bit - 2 * bit * ((x // bit) % 2)

    ids = iter(range(n_copies))
    pending = []

    def copy(src, dst, device, back=0):
        k = next(ids)
        return pltpu.make_async_remote_copy(
            src_ref=src, dst_ref=dst, send_sem=send_sem.at[k], recv_sem=recv_sem.at[k - back],
            device_id=device, device_id_type=MESH)

    def when(cond, act):
        if cond is None:
            act()
        else:
            pl.when(cond)(act)

    def start(copies, cond=None):
        when(cond, lambda: [c.start() for c in copies] and None)
        pending.append((copies, cond))

    def arrive(copies, cond=None):
        when(cond, lambda: [c.wait_recv() for c in copies] and None)

    def depart(copies, cond):
        pending[:] = [p for p in pending if p[0] is not copies or p[1] is not cond]
        when(cond, lambda: [c.wait_send() for c in copies] and None)

    def at(piece):
        return pl.ds(pl.multiple_of(piece * depth, depth), depth)

    def b_view(q, piece, c):
        return b_full.at[q, c, at(piece)]

    def b_stage(q, c, stage):
        bit = row_bits[stage]
        offsets = [0]
        for b in row_bits[:stage]:
            offsets = offsets + [o + b for o in offsets]
        copies = []
        for o in offsets:
            owner = i
            for b in row_bits[:stage]:
                if o & b:
                    owner = flip(owner, b)
            piece = (owner + j) % rows
            src = b_view(q, piece, c)
            copies.append(copy(src, b_view(q, piece, c), {"row": flip(i, bit)}))
        return copies

    def a_view(q, lo, size, piece):
        return a_full.at[q, piece, pl.ds(lo, size)]

    def a_stage(q, lo, size, stage):
        bit = col_bits[stage]
        owners = [j]
        for b in col_bits[:stage]:
            owners = owners + [flip(o, b) for o in owners]
        copies = []
        for o in owners:
            for m in range(slots):
                piece = (i + o + cols * m) % rows
                src = a_view(q, lo, size, piece)
                copies.append(copy(src, a_view(q, lo, size, piece), {"col": flip(j, bit)}))
        return copies

    my_pieces = [(i + j + cols * m) % rows for m in range(slots)]
    to_partner = {"layer": partner}

    def z_a(lo, size):
        return [copy(a_view(0, lo, size, my_pieces[m]),
                     a_view(1, lo, size, my_pieces[m]), to_partner) for m in range(slots)]

    def z_b(c):
        return [copy(b_view(0, my_pieces[0], c), b_view(1, my_pieces[0], c), to_partner)]

    loads = [pltpu.make_async_copy(src, dst, local_sem.at[n]) for n, (src, dst) in enumerate(zip(hbm, held))]
    for load in loads:
        load.start()

    barrier = pltpu.get_barrier_semaphore()
    peers = [{"row": flip(i, b)} for b in row_bits] + [{"col": flip(j, b)} for b in col_bits]
    peers += [{"layer": (l + d) % 4} for d in (1, 2, 3)]
    for peer in peers:
        pl.semaphore_signal(barrier, inc=1, device_id=peer, device_id_type=MESH)

    for load in loads[:4]:
        load.wait()

    block = a_val.shape[-1]
    inner, tile_cols = depth // block, CHUNKS * width // block
    caps = a_val.shape[1]
    a_slot = [
        inverse([jnp.where(s < a_num[m], a_pos[m, 0, s] * inner + a_pos[m, 1, s], -1) for s in range(caps)],
                TILE_ROWS * inner, 4)
        for m in range(slots)
    ]
    b_slot = inverse(
        [jnp.where(s < b_num[0], b_pos[0, s] * tile_cols + b_pos[1, s], -1) for s in range(b_val.shape[0])],
        inner * tile_cols, 8)

    def stored(ref, slot):
        value = ref[jnp.maximum(slot - 1, 0)]
        return jnp.where(slot > 0, value, jnp.zeros_like(value))

    def a_dense():
        for m in range(slots):
            for r in range(TILE_ROWS):
                parts = [stored(a_val.at[m], a_slot[m][r * inner + k]) for k in range(inner)]
                a_full[0, my_pieces[m], pl.ds(r * block, block)] = jnp.concatenate(parts, 1)

    def b_dense(c):
        for r in range(inner):
            rows_r = pl.ds(pl.multiple_of(my_pieces[0] * depth + r * block, block), block)
            for k in range(c * width // block, (c + 1) * width // block, 2):
                parts = [stored(b_val, b_slot[r * tile_cols + k + d]) for d in range(2)]
                b_full[0, c, rows_r, pl.ds(k * block - c * width, 2 * block)] = jnp.concatenate(parts, 1)

    for load in loads[4:]:
        load.wait()
    a_dense()
    b_dense(0)
    b_dense(1)
    pl.semaphore_wait(barrier, len(peers))

    def a_finish(q, lo, size, first, cond):
        arrive(first, cond)
        for stage in range(1, len(col_bits)):
            more = a_stage(q, lo, size, stage)
            start(more, cond)
            arrive(more, cond)

    def b_relay(q, c, first, cond):
        arrive(first, cond)
        for stage in range(1, len(row_bits)):
            more = b_stage(q, c, stage)
            start(more, cond)
            if stage < len(row_bits) - 1:
                arrive(more, cond)
        return more

    step = min(rows * depth, 512)

    def steps(act):
        total = rows * depth // step
        if total == 1:
            act(pl.ds(0, step))
        else:
            pl.loop(0, total)(lambda k: act(pl.ds(pl.multiple_of(k * step, step), step)))

    def chunk(c):
        return pl.ds(c * width, width)

    def halve_a(q, n):
        def act(piece):
            k = at(piece)
            high, low = halves(a_full[q, piece, pl.ds(starts[n], part)])
            a_half[q, n, pl.ds(0, part), k] = high
            a_half[q, n, pl.ds(part, part), k] = low
        if rows <= 4:
            for piece in range(rows):
                act(piece)
        else:
            pl.loop(0, rows)(act)

    def halve_b(q, c):
        def act(k):
            b_half[q, 0, c, k], b_half[q, 1, c, k] = halves(b_full[q, c, k])
        steps(act)

    def product(layers, n, c, out):
        def term(q, k):
            first = jnp.dot(a_half[q, n, :, k], b_half[q, 0, c, k], preferred_element_type=jnp.float32)
            other = jnp.dot(a_half[q, n, pl.ds(0, part), k], b_half[q, 1, c, k], preferred_element_type=jnp.float32)
            return first[:part] + (first[part:] + other)

        if rows * depth == step:
            value = term(layers[0], pl.ds(0, step))
            for q in layers[1:]:
                value = value + term(q, pl.ds(0, step))
            out[...] = value
        else:
            out[...] = jnp.zeros((part, width), jnp.float32)
            for q in layers:
                def act(k, q=q):
                    out[...] += term(q, k)
                steps(act)

    far_sent, near_sent = [], []
    for c in range(CHUNKS):
        far_sent.append([copy(sent.at[n, c], landed.at[0, c], {"layer": dests[n]}, n) for n in range(2)])
        near_sent.append([copy(sent.at[2, c], landed.at[1, c], to_partner)])

    def far_chunk(n, c):
        when(is_inner, lambda: product((0, 1), n, c, sent.at[n, c]))
        start([far_sent[c][n]], is_inner)

    def near_chunk(c):
        when(is_inner, lambda: product((0,), 2, c, sent.at[2, c]))
        start(near_sent[c], is_inner)

    def chunk_here(c):
        arrive(last0[c])
        arrive(last1[c], is_inner)
        halve_b(0, c)
        when(is_inner, lambda: halve_b(1, c))

    def outer_chunk(c):
        when(is_outer, lambda: product((0,), 2, c, out_ref.at[:, chunk(c)]))

    za = [z_a(starts[n], part) for n in (0, 1, 3)]
    zb = [z_b(c) for c in range(CHUNKS)]
    fo0, fi0 = a_stage(0, starts[0], part, 0), a_stage(0, starts[1], part, 0)
    fo1, fi1 = a_stage(1, starts[0], part, 0), a_stage(1, starts[1], part, 0)
    near0, inner1 = a_stage(0, near_lo, 2 * part, 0), a_stage(1, starts[3], part, 0)
    b0 = [b_stage(0, c, 0) for c in range(CHUNKS)]
    b1 = [b_stage(1, c, 0) for c in range(CHUNKS)]
    last0, last1 = [None] * CHUNKS, [None] * CHUNKS

    start(za[0], is_outer)
    start(fo0, is_inner)
    start(b0[0])
    start(zb[0], is_outer)
    start(near0, is_outer)
    start(b0[1])
    for c in range(2, CHUNKS):
        b_dense(c)
    last0[0] = b_relay(0, 0, b0[0], None)
    arrive(za[0], is_inner)
    start(fo1, is_inner)
    start(fi0, is_inner)
    depart(za[0], is_outer)
    start(za[1], is_outer)
    arrive(zb[0], is_inner)
    start(b1[0], is_inner)
    depart(zb[0], is_outer)
    start(zb[1], is_outer)
    last0[1] = b_relay(0, 1, b0[1], None)
    start(b0[2])
    a_finish(0, starts[0], part, fo0, is_inner)
    a_finish(1, starts[0], part, fo1, is_inner)
    when(is_inner, lambda: [halve_a(q, 0) for q in range(2)] and None)
    last1[0] = b_relay(1, 0, b1[0], is_inner)
    arrive(za[1], is_inner)
    start(fi1, is_inner)
    start(near0, is_inner)
    depart(za[1], is_outer)
    start(zb[2], is_outer)
    chunk_here(0)
    far_chunk(0, 0)
    arrive(zb[1], is_inner)
    start(b1[1], is_inner)
    depart(zb[1], is_outer)
    start(zb[3], is_outer)
    a_finish(0, starts[1], part, fi0, is_inner)
    a_finish(1, starts[1], part, fi1, is_inner)
    when(is_inner, lambda: [halve_a(q, 1) for q in range(2)] and None)
    far_chunk(1, 0)
    last0[2] = b_relay(0, 2, b0[2], None)
    start(b0[3])
    arrive(zb[2], is_inner)
    start(b1[2], is_inner)
    depart(zb[2], is_outer)
    start(za[2], is_outer)
    last1[1] = b_relay(1, 1, b1[1], is_inner)
    chunk_here(1)
    far_chunk(0, 1)
    far_chunk(1, 1)
    arrive(zb[3], is_inner)
    start(b1[3], is_inner)
    a_finish(0, near_lo, 2 * part, near0, None)
    halve_a(0, 2)
    when(is_inner, lambda: halve_a(0, 3))
    near_chunk(0)
    outer_chunk(0)
    outer_chunk(1)
    last0[3] = b_relay(0, 3, b0[3], None)
    last1[2] = b_relay(1, 2, b1[2], is_inner)
    chunk_here(2)
    far_chunk(0, 2)
    far_chunk(1, 2)
    near_chunk(1)
    outer_chunk(2)
    arrive(za[2], is_inner)
    start(inner1, is_inner)
    last1[3] = b_relay(1, 3, b1[3], is_inner)
    chunk_here(3)
    far_chunk(0, 3)
    far_chunk(1, 3)
    near_chunk(2)
    near_chunk(3)
    outer_chunk(3)
    a_finish(1, starts[3], part, inner1, is_inner)
    when(is_inner, lambda: halve_a(1, 3))
    for c in range(CHUNKS):
        when(is_inner, lambda c=c: product((0, 1), 3, c, out_ref.at[:, chunk(c)]))
    for c in range(CHUNKS):
        far_sent[c][0].wait_recv()
        out_ref[:, chunk(c)] += landed[0, c]

        def add(c=c):
            near_sent[c][0].wait_recv()
            out_ref[:, chunk(c)] += landed[1, c]
        when(is_outer, add)
    for copies, cond in list(pending):
        depart(copies, cond)


def body(rows, cols, a_values, a_places, a_counts, b_values, b_places, b_counts):
    a_vals = a_values.reshape(a_values.shape[3:])
    b_vals = b_values.reshape(b_values.shape[3:])
    slots, block = a_vals.shape[0], a_vals.shape[2]
    layers = lax.axis_size("layer")
    inner = TILE_ROWS // layers
    tile_cols = TILE_ROWS * rows // cols
    a_pos = jnp.swapaxes(a_places.reshape(a_places.shape[3:]), 1, 2)
    a_num = a_counts.reshape(slots)
    b_pos = b_places.reshape(b_places.shape[3:]).T
    b_num = b_counts.reshape(1)
    depth, part = inner * block, TILE_ROWS * block // layers
    full_rows, full_cols = TILE_ROWS * block, tile_cols * block
    width = full_cols // CHUNKS
    f32 = jnp.float32
    vmem = pl.BlockSpec(memory_space=pltpu.VMEM)
    n_copies = 2 * CHUNKS * (rows - 1) + 6 * slots * (cols - 1) + 3 * slots + 4 * CHUNKS
    return pl.pallas_call(
        functools.partial(multiply, rows, cols, part, depth, n_copies),
        out_shape=jax.ShapeDtypeStruct((part, full_cols), f32),
        in_specs=[pl.BlockSpec(memory_space=pltpu.HBM)] * 6,
        out_specs=vmem,
        scratch_shapes=[
            *[pltpu.SMEM(x.shape, jnp.int32) for x in (a_pos, a_num, b_pos, b_num)],
            pltpu.VMEM(a_vals.shape, f32),
            pltpu.VMEM(b_vals.shape, f32),
            pltpu.VMEM((2, rows, full_rows, depth), f32),
            pltpu.VMEM((2, CHUNKS, rows * depth, width), f32),
            pltpu.VMEM((2, layers, 2 * part, rows * depth), jnp.bfloat16),
            pltpu.VMEM((2, 2, CHUNKS, rows * depth, width), jnp.bfloat16),
            pltpu.VMEM((3, CHUNKS, part, width), f32),
            pltpu.VMEM((2, CHUNKS, part, width), f32),
            pltpu.SemaphoreType.DMA((n_copies,)),
            pltpu.SemaphoreType.DMA((n_copies,)),
            pltpu.SemaphoreType.DMA((6,)),
        ],
        compiler_params=pltpu.CompilerParams(collective_id=0, has_side_effects=True, vmem_limit_bytes=63 * 2**20),
    )(a_pos, a_num, b_pos, b_num, a_vals, b_vals)


def solution(mesh):
    in_specs = (
        P("row", "col", "layer", None, None, None, None),
        P("row", "col", "layer", None, None, None),
        P("row", "col", "layer", None),
        P("row", "col", "layer", None, None, None),
        P("row", "col", "layer", None, None),
        P("row", "col", "layer"),
    )
    out_specs = P(("row", "layer"), "col")
    call = functools.partial(body, mesh.shape["row"], mesh.shape["col"])
    return jax.shard_map(call, mesh=mesh, in_specs=in_specs, out_specs=out_specs, check_vma=False)
```

```python
import functools

import jax
import jax.numpy as jnp
from jax import lax
from jax.experimental import pallas as pl
from jax.experimental.pallas import tpu as pltpu
from jax.sharding import PartitionSpec as P

MESH = pl.DeviceIdType.MESH
TILE_ROWS = 8


def chunk_widths(total):
    unit = total // 8
    return [unit] + [2 * unit] * 3 + [unit]


def inverse(spots, total, bits):
    each = 32 // bits
    words = [jnp.int32(0)] * (-(-total // each))
    for s, spot in enumerate(spots):
        mark = jnp.left_shift(jnp.int32(s + 1), bits * (spot % each))
        for w in range(len(words)):
            inside = jnp.logical_and(spot >= w * each, spot < (w + 1) * each)
            words[w] = words[w] + jnp.where(inside, mark, 0)
    return [jnp.right_shift(words[t // each], bits * (t % each)) & (2**bits - 1) for t in range(total)]


def halves(x):
    high = x.astype(jnp.bfloat16)
    return high, (x - high.astype(jnp.float32)).astype(jnp.bfloat16)


def powers(n):
    out, b = [], n // 2
    while b:
        out.append(b)
        b //= 2
    return out


def multiply(rows, cols, part, depth, n_copies, *refs):
    hbm, out_ref, held = refs[:6], refs[6], refs[7:13]
    a_pos, a_num, b_pos, b_num, a_val, b_val = held
    a_full, b_full, a_half, b_half, sent, landed, send_sem, recv_sem, local_sem = refs[13:]
    i, j, l = lax.axis_index("row"), lax.axis_index("col"), lax.axis_index("layer")
    row_bits, col_bits = powers(rows), powers(cols)
    slots = rows // cols
    widths = chunk_widths(b_full.shape[2])
    n_chunks = len(widths)
    partner = l + 1 - 2 * (l % 2)
    is_inner = jnp.logical_or(l == 1, l == 2)
    is_outer = jnp.logical_or(l == 0, l == 3)
    inner_dest = 1 + l // 2
    outer_dest = 3 * (l // 2)
    dests = [3 - 3 * (l // 2), 2 - l // 2, outer_dest, inner_dest]
    starts = [pl.multiple_of(part * dest, part) for dest in dests]
    near_lo = pl.multiple_of(2 * part * (l // 2), 2 * part)

    def flip(x, bit):
        return x + bit - 2 * bit * ((x // bit) % 2)

    ids = iter(range(n_copies))
    pending = []

    def copy(src, dst, device, back=0):
        k = next(ids)
        return pltpu.make_async_remote_copy(
            src_ref=src, dst_ref=dst, send_sem=send_sem.at[k], recv_sem=recv_sem.at[k - back],
            device_id=device, device_id_type=MESH)

    def when(cond, act):
        if cond is None:
            act()
        else:
            pl.when(cond)(act)

    def start(copies, cond=None):
        when(cond, lambda: [c.start() for c in copies] and None)
        pending.append((copies, cond))

    def arrive(copies, cond=None):
        when(cond, lambda: [c.wait_recv() for c in copies] and None)

    def depart(copies, cond):
        pending[:] = [p for p in pending if p[0] is not copies or p[1] is not cond]
        when(cond, lambda: [c.wait_send() for c in copies] and None)

    def at(piece):
        return pl.ds(pl.multiple_of(piece * depth, depth), depth)

    def b_view(q, piece, c):
        return b_full.at[q, at(piece), chunk(c)]

    def chunk(c):
        return pl.ds(sum(widths[:c]), widths[c])

    def b_stage(q, c, stage):
        bit = row_bits[stage]
        offsets = [0]
        for b in row_bits[:stage]:
            offsets = offsets + [o + b for o in offsets]
        copies = []
        for o in offsets:
            owner = i
            for b in row_bits[:stage]:
                if o & b:
                    owner = flip(owner, b)
            piece = (owner + j) % rows
            src = b_view(q, piece, c)
            copies.append(copy(src, b_view(q, piece, c), {"row": flip(i, bit)}))
        return copies

    def a_view(q, lo, size, piece):
        return a_full.at[q, piece, pl.ds(lo, size)]

    def a_stage(q, lo, size, stage):
        bit = col_bits[stage]
        owners = [j]
        for b in col_bits[:stage]:
            owners = owners + [flip(o, b) for o in owners]
        copies = []
        for o in owners:
            for m in range(slots):
                piece = (i + o + cols * m) % rows
                src = a_view(q, lo, size, piece)
                copies.append(copy(src, a_view(q, lo, size, piece), {"col": flip(j, bit)}))
        return copies

    my_pieces = [(i + j + cols * m) % rows for m in range(slots)]
    to_partner = {"layer": partner}

    def z_a(lo, size):
        return [copy(a_view(0, lo, size, my_pieces[m]),
                     a_view(1, lo, size, my_pieces[m]), to_partner) for m in range(slots)]

    def z_b(c):
        return [copy(b_view(0, my_pieces[0], c), b_view(1, my_pieces[0], c), to_partner)]

    loads = [pltpu.make_async_copy(src, dst, local_sem.at[n]) for n, (src, dst) in enumerate(zip(hbm, held))]
    for load in loads:
        load.start()

    barrier = pltpu.get_barrier_semaphore()
    peers = [{"row": flip(i, b)} for b in row_bits] + [{"col": flip(j, b)} for b in col_bits]
    peers += [{"layer": (l + d) % 4} for d in (1, 2, 3)]
    for peer in peers:
        pl.semaphore_signal(barrier, inc=1, device_id=peer, device_id_type=MESH)

    for load in loads[:4]:
        load.wait()

    block = a_val.shape[-1]
    inner, tile_cols = depth // block, b_full.shape[2] // block
    caps = a_val.shape[1]
    a_slot = [
        inverse([jnp.where(s < a_num[m], a_pos[m, 0, s] * inner + a_pos[m, 1, s], -1) for s in range(caps)],
                TILE_ROWS * inner, 4)
        for m in range(slots)
    ]
    b_slot = inverse(
        [jnp.where(s < b_num[0], b_pos[0, s] * tile_cols + b_pos[1, s], -1) for s in range(b_val.shape[0])],
        inner * tile_cols, 8)

    def stored(ref, slot):
        value = ref[jnp.maximum(slot - 1, 0)]
        return jnp.where(slot > 0, value, jnp.zeros_like(value))

    def a_dense():
        for m in range(slots):
            for r in range(TILE_ROWS):
                parts = [stored(a_val.at[m], a_slot[m][r * inner + k]) for k in range(inner)]
                a_full[0, my_pieces[m], pl.ds(r * block, block)] = jnp.concatenate(parts, 1)

    def b_dense(c):
        for r in range(inner):
            rows_r = pl.ds(pl.multiple_of(my_pieces[0] * depth + r * block, block), block)
            for k in range(sum(widths[:c]) // block, sum(widths[:c + 1]) // block, 2):
                parts = [stored(b_val, b_slot[r * tile_cols + k + d]) for d in range(2)]
                b_full[0, rows_r, pl.ds(k * block, 2 * block)] = jnp.concatenate(parts, 1)

    for load in loads[4:]:
        load.wait()
    a_dense()
    b_dense(0)
    b_dense(1)
    pl.semaphore_wait(barrier, len(peers))

    def a_finish(q, lo, size, first, cond):
        arrive(first, cond)
        for stage in range(1, len(col_bits)):
            more = a_stage(q, lo, size, stage)
            start(more, cond)
            arrive(more, cond)

    def b_relay(q, c, first, cond):
        arrive(first, cond)
        for stage in range(1, len(row_bits)):
            more = b_stage(q, c, stage)
            start(more, cond)
            if stage < len(row_bits) - 1:
                arrive(more, cond)
        return more

    step = min(rows * depth, 512)

    def steps(act):
        total = rows * depth // step
        if total == 1:
            act(pl.ds(0, step))
        else:
            pl.loop(0, total)(lambda k: act(pl.ds(pl.multiple_of(k * step, step), step)))

    def halve_a(q, n):
        def act(piece):
            k = at(piece)
            high, low = halves(a_full[q, piece, pl.ds(starts[n], part)])
            a_half[q, n, pl.ds(0, part), k] = high
            a_half[q, n, pl.ds(part, part), k] = low
        if rows <= 4:
            for piece in range(rows):
                act(piece)
        else:
            pl.loop(0, rows)(act)

    def halve_b(q, c):
        def act(k):
            b_half[q, 0, k, chunk(c)], b_half[q, 1, k, chunk(c)] = halves(b_full[q, k, chunk(c)])
        steps(act)

    def product(layers, n, c, out):
        def term(q, k):
            first = jnp.dot(a_half[q, n, :, k], b_half[q, 0, k, chunk(c)], preferred_element_type=jnp.float32)
            other = jnp.dot(a_half[q, n, pl.ds(0, part), k], b_half[q, 1, k, chunk(c)], preferred_element_type=jnp.float32)
            return first[:part] + (first[part:] + other)

        if rows * depth == step:
            value = term(layers[0], pl.ds(0, step))
            for q in layers[1:]:
                value = value + term(q, pl.ds(0, step))
            out[...] = value
        else:
            out[...] = jnp.zeros((part, widths[c]), jnp.float32)
            for q in layers:
                def act(k, q=q):
                    out[...] += term(q, k)
                steps(act)

    far_sent, near_sent = [], []
    for c in range(n_chunks):
        far_sent.append([copy(sent.at[n, :, chunk(c)], landed.at[0, :, chunk(c)], {"layer": dests[n]}, n) for n in range(2)])
        near_sent.append([copy(sent.at[2, :, chunk(c)], landed.at[1, :, chunk(c)], to_partner)])

    def far_chunk(n, c):
        when(is_inner, lambda: product((0, 1), n, c, sent.at[n, :, chunk(c)]))
        start([far_sent[c][n]], is_inner)

    def near_chunk(c):
        when(is_inner, lambda: product((0,), 2, c, sent.at[2, :, chunk(c)]))
        start(near_sent[c], is_inner)

    def chunk_here(c):
        arrive(last0[c])
        arrive(last1[c], is_inner)
        halve_b(0, c)
        when(is_inner, lambda: halve_b(1, c))

    def outer_chunk(c):
        when(is_outer, lambda: product((0,), 2, c, out_ref.at[:, chunk(c)]))

    za = [z_a(starts[n], part) for n in (0, 1, 3)]
    zb = [z_b(c) for c in range(n_chunks)]
    fo0, fi0 = a_stage(0, starts[0], part, 0), a_stage(0, starts[1], part, 0)
    fo1, fi1 = a_stage(1, starts[0], part, 0), a_stage(1, starts[1], part, 0)
    near0, inner1 = a_stage(0, near_lo, 2 * part, 0), a_stage(1, starts[3], part, 0)
    b0 = [b_stage(0, c, 0) for c in range(n_chunks)]
    b1 = [b_stage(1, c, 0) for c in range(n_chunks)]
    last0, last1 = [None] * n_chunks, [None] * n_chunks

    z_queue = [za[0], zb[0], za[1]] + zb[1:] + [za[2]]
    z_started = []

    def more_z():
        if len(z_started) >= 2:
            depart(z_started[-2], is_outer)
        if len(z_started) < len(z_queue):
            start(z_queue[len(z_started)], is_outer)
            z_started.append(z_queue[len(z_started)])

    more_z()
    start(fo0, is_inner)
    start(b0[0])
    more_z()
    start(near0, is_outer)
    start(b0[1])
    for c in range(2, n_chunks):
        b_dense(c)
    last0[0] = b_relay(0, 0, b0[0], None)
    arrive(za[0], is_inner)
    start(fo1, is_inner)
    start(fi0, is_inner)
    more_z()
    arrive(zb[0], is_inner)
    start(b1[0], is_inner)
    more_z()
    last0[1] = b_relay(0, 1, b0[1], None)
    start(b0[2])
    a_finish(0, starts[0], part, fo0, is_inner)
    a_finish(1, starts[0], part, fo1, is_inner)
    when(is_inner, lambda: [halve_a(q, 0) for q in range(2)] and None)
    last1[0] = b_relay(1, 0, b1[0], is_inner)
    arrive(za[1], is_inner)
    start(fi1, is_inner)
    start(near0, is_inner)
    more_z()
    chunk_here(0)
    far_chunk(0, 0)
    arrive(zb[1], is_inner)
    start(b1[1], is_inner)
    more_z()
    a_finish(0, starts[1], part, fi0, is_inner)
    a_finish(1, starts[1], part, fi1, is_inner)
    when(is_inner, lambda: [halve_a(q, 1) for q in range(2)] and None)
    far_chunk(1, 0)
    for c in range(1, n_chunks):
        if c + 1 < n_chunks:
            last0[c + 1] = b_relay(0, c + 1, b0[c + 1], None)
            if c + 2 < n_chunks:
                start(b0[c + 2])
            arrive(zb[c + 1], is_inner)
            start(b1[c + 1], is_inner)
            more_z()
        else:
            arrive(za[2], is_inner)
            start(inner1, is_inner)
        last1[c] = b_relay(1, c, b1[c], is_inner)
        chunk_here(c)
        far_chunk(0, c)
        far_chunk(1, c)
        if c == 2:
            a_finish(0, near_lo, 2 * part, near0, None)
            halve_a(0, 2)
            when(is_inner, lambda: halve_a(0, 3))
        if c >= 2:
            near_chunk(c - 2)
            outer_chunk(c - 2)
    for c in range(n_chunks - 2, n_chunks):
        near_chunk(c)
        outer_chunk(c)
    a_finish(1, starts[3], part, inner1, is_inner)
    when(is_inner, lambda: halve_a(1, 3))
    for c in range(n_chunks):
        when(is_inner, lambda c=c: product((0, 1), 3, c, out_ref.at[:, chunk(c)]))
    for c in range(n_chunks):
        far_sent[c][0].wait_recv()
        out_ref[:, chunk(c)] += landed[0, :, chunk(c)]

        def add(c=c):
            near_sent[c][0].wait_recv()
            out_ref[:, chunk(c)] += landed[1, :, chunk(c)]
        when(is_outer, add)
    for copies, cond in list(pending):
        depart(copies, cond)


def body(rows, cols, a_values, a_places, a_counts, b_values, b_places, b_counts):
    a_vals = a_values.reshape(a_values.shape[3:])
    b_vals = b_values.reshape(b_values.shape[3:])
    slots, block = a_vals.shape[0], a_vals.shape[2]
    layers = lax.axis_size("layer")
    inner = TILE_ROWS // layers
    tile_cols = TILE_ROWS * rows // cols
    a_pos = jnp.swapaxes(a_places.reshape(a_places.shape[3:]), 1, 2)
    a_num = a_counts.reshape(slots)
    b_pos = b_places.reshape(b_places.shape[3:]).T
    b_num = b_counts.reshape(1)
    depth, part = inner * block, TILE_ROWS * block // layers
    full_rows, full_cols = TILE_ROWS * block, tile_cols * block
    chunks = len(chunk_widths(full_cols))
    f32 = jnp.float32
    vmem = pl.BlockSpec(memory_space=pltpu.VMEM)
    n_copies = 2 * chunks * (rows - 1) + 6 * slots * (cols - 1) + 3 * slots + 4 * chunks
    return pl.pallas_call(
        functools.partial(multiply, rows, cols, part, depth, n_copies),
        out_shape=jax.ShapeDtypeStruct((part, full_cols), f32),
        in_specs=[pl.BlockSpec(memory_space=pltpu.HBM)] * 6,
        out_specs=vmem,
        scratch_shapes=[
            *[pltpu.SMEM(x.shape, jnp.int32) for x in (a_pos, a_num, b_pos, b_num)],
            pltpu.VMEM(a_vals.shape, f32),
            pltpu.VMEM(b_vals.shape, f32),
            pltpu.VMEM((2, rows, full_rows, depth), f32),
            pltpu.VMEM((2, rows * depth, full_cols), f32),
            pltpu.VMEM((2, layers, 2 * part, rows * depth), jnp.bfloat16),
            pltpu.VMEM((2, 2, rows * depth, full_cols), jnp.bfloat16),
            pltpu.VMEM((3, part, full_cols), f32),
            pltpu.VMEM((2, part, full_cols), f32),
            pltpu.SemaphoreType.DMA((n_copies,)),
            pltpu.SemaphoreType.DMA((n_copies,)),
            pltpu.SemaphoreType.DMA((6,)),
        ],
        compiler_params=pltpu.CompilerParams(collective_id=0, has_side_effects=True, vmem_limit_bytes=63 * 2**20),
    )(a_pos, a_num, b_pos, b_num, a_vals, b_vals)


def solution(mesh):
    in_specs = (
        P("row", "col", "layer", None, None, None, None),
        P("row", "col", "layer", None, None, None),
        P("row", "col", "layer", None),
        P("row", "col", "layer", None, None, None),
        P("row", "col", "layer", None, None),
        P("row", "col", "layer"),
    )
    out_specs = P(("row", "layer"), "col")
    call = functools.partial(body, mesh.shape["row"], mesh.shape["col"])
    return jax.shard_map(call, mesh=mesh, in_specs=in_specs, out_specs=out_specs, check_vma=False)
```

```python
import functools

import jax
import jax.numpy as jnp
from jax import lax
from jax.experimental import pallas as pl
from jax.experimental.pallas import tpu as pltpu
from jax.sharding import PartitionSpec as P

MESH = pl.DeviceIdType.MESH
TILE_ROWS = 8


def chunk_widths(total):
    unit = total // 4
    return [unit, 2 * unit, unit]


def inverse(spots, total, bits):
    each = 32 // bits
    words = [jnp.int32(0)] * (-(-total // each))
    for s, spot in enumerate(spots):
        mark = jnp.left_shift(jnp.int32(s + 1), bits * (spot % each))
        for w in range(len(words)):
            inside = jnp.logical_and(spot >= w * each, spot < (w + 1) * each)
            words[w] = words[w] + jnp.where(inside, mark, 0)
    return [jnp.right_shift(words[t // each], bits * (t % each)) & (2**bits - 1) for t in range(total)]


def halves(x):
    high = x.astype(jnp.bfloat16)
    return high, (x - high.astype(jnp.float32)).astype(jnp.bfloat16)


def powers(n):
    out, b = [], n // 2
    while b:
        out.append(b)
        b //= 2
    return out


def multiply(rows, cols, part, depth, n_copies, *refs):
    hbm, out_ref, held = refs[:6], refs[6], refs[7:13]
    a_pos, a_num, b_pos, b_num, a_val, b_val = held
    a_full, b_full, a_half, b_half, sent, landed, send_sem, recv_sem, local_sem = refs[13:]
    i, j, l = lax.axis_index("row"), lax.axis_index("col"), lax.axis_index("layer")
    row_bits, col_bits = powers(rows), powers(cols)
    slots = rows // cols
    widths = chunk_widths(b_full.shape[2])
    n_chunks = len(widths)
    partner = l + 1 - 2 * (l % 2)
    is_inner = jnp.logical_or(l == 1, l == 2)
    is_outer = jnp.logical_or(l == 0, l == 3)
    inner_dest = 1 + l // 2
    outer_dest = 3 * (l // 2)
    dests = [3 - 3 * (l // 2), 2 - l // 2, outer_dest, inner_dest]
    starts = [pl.multiple_of(part * dest, part) for dest in dests]
    near_lo = pl.multiple_of(2 * part * (l // 2), 2 * part)

    def flip(x, bit):
        return x + bit - 2 * bit * ((x // bit) % 2)

    ids = iter(range(n_copies))
    pending = []

    def copy(src, dst, device, back=0):
        k = next(ids)
        return pltpu.make_async_remote_copy(
            src_ref=src, dst_ref=dst, send_sem=send_sem.at[k], recv_sem=recv_sem.at[k - back],
            device_id=device, device_id_type=MESH)

    def when(cond, act):
        if cond is None:
            act()
        else:
            pl.when(cond)(act)

    def start(copies, cond=None):
        when(cond, lambda: [c.start() for c in copies] and None)
        pending.append((copies, cond))

    def arrive(copies, cond=None):
        when(cond, lambda: [c.wait_recv() for c in copies] and None)

    def depart(copies, cond):
        pending[:] = [p for p in pending if p[0] is not copies or p[1] is not cond]
        when(cond, lambda: [c.wait_send() for c in copies] and None)

    def at(piece):
        return pl.ds(pl.multiple_of(piece * depth, depth), depth)

    def b_view(q, piece, c):
        return b_full.at[q, at(piece), chunk(c)]

    def chunk(c):
        return pl.ds(sum(widths[:c]), widths[c])

    def b_stage(q, c, stage):
        bit = row_bits[stage]
        offsets = [0]
        for b in row_bits[:stage]:
            offsets = offsets + [o + b for o in offsets]
        copies = []
        for o in offsets:
            owner = i
            for b in row_bits[:stage]:
                if o & b:
                    owner = flip(owner, b)
            piece = (owner + j) % rows
            src = b_view(q, piece, c)
            copies.append(copy(src, b_view(q, piece, c), {"row": flip(i, bit)}))
        return copies

    def a_view(q, lo, size, piece):
        return a_full.at[q, piece, pl.ds(lo, size)]

    def a_stage(q, lo, size, stage):
        bit = col_bits[stage]
        owners = [j]
        for b in col_bits[:stage]:
            owners = owners + [flip(o, b) for o in owners]
        copies = []
        for o in owners:
            for m in range(slots):
                piece = (i + o + cols * m) % rows
                src = a_view(q, lo, size, piece)
                copies.append(copy(src, a_view(q, lo, size, piece), {"col": flip(j, bit)}))
        return copies

    my_pieces = [(i + j + cols * m) % rows for m in range(slots)]
    to_partner = {"layer": partner}

    def z_a(lo, size):
        return [copy(a_view(0, lo, size, my_pieces[m]),
                     a_view(1, lo, size, my_pieces[m]), to_partner) for m in range(slots)]

    def z_b(c):
        return [copy(b_view(0, my_pieces[0], c), b_view(1, my_pieces[0], c), to_partner)]

    loads = [pltpu.make_async_copy(src, dst, local_sem.at[n]) for n, (src, dst) in enumerate(zip(hbm, held))]
    for load in loads:
        load.start()

    barrier = pltpu.get_barrier_semaphore()
    peers = [{"row": flip(i, b)} for b in row_bits] + [{"col": flip(j, b)} for b in col_bits]
    peers += [{"layer": (l + d) % 4} for d in (1, 2, 3)]
    for peer in peers:
        pl.semaphore_signal(barrier, inc=1, device_id=peer, device_id_type=MESH)

    for load in loads[:4]:
        load.wait()

    block = a_val.shape[-1]
    inner, tile_cols = depth // block, b_full.shape[2] // block
    caps = a_val.shape[1]
    a_slot = [
        inverse([jnp.where(s < a_num[m], a_pos[m, 0, s] * inner + a_pos[m, 1, s], -1) for s in range(caps)],
                TILE_ROWS * inner, 4)
        for m in range(slots)
    ]
    b_slot = inverse(
        [jnp.where(s < b_num[0], b_pos[0, s] * tile_cols + b_pos[1, s], -1) for s in range(b_val.shape[0])],
        inner * tile_cols, 8)

    def stored(ref, slot):
        value = ref[jnp.maximum(slot - 1, 0)]
        return jnp.where(slot > 0, value, jnp.zeros_like(value))

    def a_dense():
        for m in range(slots):
            for r in range(TILE_ROWS):
                parts = [stored(a_val.at[m], a_slot[m][r * inner + k]) for k in range(inner)]
                a_full[0, my_pieces[m], pl.ds(r * block, block)] = jnp.concatenate(parts, 1)

    def b_dense(c):
        for r in range(inner):
            rows_r = pl.ds(pl.multiple_of(my_pieces[0] * depth + r * block, block), block)
            for k in range(sum(widths[:c]) // block, sum(widths[:c + 1]) // block, 2):
                parts = [stored(b_val, b_slot[r * tile_cols + k + d]) for d in range(2)]
                b_full[0, rows_r, pl.ds(k * block, 2 * block)] = jnp.concatenate(parts, 1)

    for load in loads[4:]:
        load.wait()
    a_dense()
    b_dense(0)
    b_dense(1)
    pl.semaphore_wait(barrier, len(peers))

    def a_finish(q, lo, size, first, cond):
        arrive(first, cond)
        for stage in range(1, len(col_bits)):
            more = a_stage(q, lo, size, stage)
            start(more, cond)
            arrive(more, cond)

    def b_relay(q, c, first, cond):
        arrive(first, cond)
        for stage in range(1, len(row_bits)):
            more = b_stage(q, c, stage)
            start(more, cond)
            if stage < len(row_bits) - 1:
                arrive(more, cond)
        return more

    step = min(rows * depth, 512)

    def steps(act):
        total = rows * depth // step
        if total == 1:
            act(pl.ds(0, step))
        else:
            pl.loop(0, total)(lambda k: act(pl.ds(pl.multiple_of(k * step, step), step)))

    def halve_a(q, n):
        def act(piece):
            k = at(piece)
            high, low = halves(a_full[q, piece, pl.ds(starts[n], part)])
            a_half[q, n, pl.ds(0, part), k] = high
            a_half[q, n, pl.ds(part, part), k] = low
        if rows <= 4:
            for piece in range(rows):
                act(piece)
        else:
            pl.loop(0, rows)(act)

    def halve_b(q, c):
        def act(k):
            b_half[q, 0, k, chunk(c)], b_half[q, 1, k, chunk(c)] = halves(b_full[q, k, chunk(c)])
        steps(act)

    def product(layers, n, c, out):
        def term(q, k):
            first = jnp.dot(a_half[q, n, :, k], b_half[q, 0, k, chunk(c)], preferred_element_type=jnp.float32)
            other = jnp.dot(a_half[q, n, pl.ds(0, part), k], b_half[q, 1, k, chunk(c)], preferred_element_type=jnp.float32)
            return first[:part] + (first[part:] + other)

        if rows * depth == step:
            value = term(layers[0], pl.ds(0, step))
            for q in layers[1:]:
                value = value + term(q, pl.ds(0, step))
            out[...] = value
        else:
            out[...] = jnp.zeros((part, widths[c]), jnp.float32)
            for q in layers:
                def act(k, q=q):
                    out[...] += term(q, k)
                steps(act)

    far_sent, near_sent = [], []
    for c in range(n_chunks):
        far_sent.append([copy(sent.at[n, :, chunk(c)], landed.at[0, :, chunk(c)], {"layer": dests[n]}, n) for n in range(2)])
        near_sent.append([copy(sent.at[2, :, chunk(c)], landed.at[1, :, chunk(c)], to_partner)])

    def far_chunk(n, c):
        when(is_inner, lambda: product((0, 1), n, c, sent.at[n, :, chunk(c)]))
        start([far_sent[c][n]], is_inner)

    def near_chunk(c):
        when(is_inner, lambda: product((0,), 2, c, sent.at[2, :, chunk(c)]))
        start(near_sent[c], is_inner)

    def chunk_here(c):
        arrive(last0[c])
        arrive(last1[c], is_inner)
        halve_b(0, c)
        when(is_inner, lambda: halve_b(1, c))

    def outer_chunk(c):
        when(is_outer, lambda: product((0,), 2, c, out_ref.at[:, chunk(c)]))

    za = [z_a(starts[n], part) for n in (0, 1, 3)]
    zb = [z_b(c) for c in range(n_chunks)]
    fo0, fi0 = a_stage(0, starts[0], part, 0), a_stage(0, starts[1], part, 0)
    fo1, fi1 = a_stage(1, starts[0], part, 0), a_stage(1, starts[1], part, 0)
    near0, inner1 = a_stage(0, near_lo, 2 * part, 0), a_stage(1, starts[3], part, 0)
    b0 = [b_stage(0, c, 0) for c in range(n_chunks)]
    b1 = [b_stage(1, c, 0) for c in range(n_chunks)]
    last0, last1 = [None] * n_chunks, [None] * n_chunks

    z_queue = [za[0], zb[0], za[1]] + zb[1:] + [za[2]]
    z_started = []

    def more_z():
        if len(z_started) >= 2:
            depart(z_started[-2], is_outer)
        if len(z_started) < len(z_queue):
            start(z_queue[len(z_started)], is_outer)
            z_started.append(z_queue[len(z_started)])

    more_z()
    start(fo0, is_inner)
    start(b0[0])
    more_z()
    start(near0, is_outer)
    start(b0[1])
    for c in range(2, n_chunks):
        b_dense(c)
    last0[0] = b_relay(0, 0, b0[0], None)
    arrive(za[0], is_inner)
    start(fo1, is_inner)
    start(fi0, is_inner)
    more_z()
    arrive(zb[0], is_inner)
    start(b1[0], is_inner)
    more_z()
    last0[1] = b_relay(0, 1, b0[1], None)
    start(b0[2])
    a_finish(0, starts[0], part, fo0, is_inner)
    a_finish(1, starts[0], part, fo1, is_inner)
    when(is_inner, lambda: [halve_a(q, 0) for q in range(2)] and None)
    last1[0] = b_relay(1, 0, b1[0], is_inner)
    arrive(za[1], is_inner)
    start(fi1, is_inner)
    start(near0, is_inner)
    more_z()
    chunk_here(0)
    far_chunk(0, 0)
    arrive(zb[1], is_inner)
    start(b1[1], is_inner)
    more_z()
    a_finish(0, starts[1], part, fi0, is_inner)
    a_finish(1, starts[1], part, fi1, is_inner)
    when(is_inner, lambda: [halve_a(q, 1) for q in range(2)] and None)
    far_chunk(1, 0)
    for c in range(1, n_chunks):
        if c + 1 < n_chunks:
            last0[c + 1] = b_relay(0, c + 1, b0[c + 1], None)
            if c + 2 < n_chunks:
                start(b0[c + 2])
            arrive(zb[c + 1], is_inner)
            start(b1[c + 1], is_inner)
            more_z()
        else:
            arrive(za[2], is_inner)
            start(inner1, is_inner)
        last1[c] = b_relay(1, c, b1[c], is_inner)
        chunk_here(c)
        far_chunk(0, c)
        far_chunk(1, c)
        if c == 2:
            a_finish(0, near_lo, 2 * part, near0, None)
            halve_a(0, 2)
            when(is_inner, lambda: halve_a(0, 3))
        if c >= 2:
            near_chunk(c - 2)
            outer_chunk(c - 2)
    for c in range(n_chunks - 2, n_chunks):
        near_chunk(c)
        outer_chunk(c)
    a_finish(1, starts[3], part, inner1, is_inner)
    when(is_inner, lambda: halve_a(1, 3))
    for c in range(n_chunks):
        when(is_inner, lambda c=c: product((0, 1), 3, c, out_ref.at[:, chunk(c)]))
    for c in range(n_chunks):
        far_sent[c][0].wait_recv()
        out_ref[:, chunk(c)] += landed[0, :, chunk(c)]

        def add(c=c):
            near_sent[c][0].wait_recv()
            out_ref[:, chunk(c)] += landed[1, :, chunk(c)]
        when(is_outer, add)
    for copies, cond in list(pending):
        depart(copies, cond)


def body(rows, cols, a_values, a_places, a_counts, b_values, b_places, b_counts):
    a_vals = a_values.reshape(a_values.shape[3:])
    b_vals = b_values.reshape(b_values.shape[3:])
    slots, block = a_vals.shape[0], a_vals.shape[2]
    layers = lax.axis_size("layer")
    inner = TILE_ROWS // layers
    tile_cols = TILE_ROWS * rows // cols
    a_pos = jnp.swapaxes(a_places.reshape(a_places.shape[3:]), 1, 2)
    a_num = a_counts.reshape(slots)
    b_pos = b_places.reshape(b_places.shape[3:]).T
    b_num = b_counts.reshape(1)
    depth, part = inner * block, TILE_ROWS * block // layers
    full_rows, full_cols = TILE_ROWS * block, tile_cols * block
    chunks = len(chunk_widths(full_cols))
    f32 = jnp.float32
    vmem = pl.BlockSpec(memory_space=pltpu.VMEM)
    n_copies = 2 * chunks * (rows - 1) + 6 * slots * (cols - 1) + 3 * slots + 4 * chunks
    return pl.pallas_call(
        functools.partial(multiply, rows, cols, part, depth, n_copies),
        out_shape=jax.ShapeDtypeStruct((part, full_cols), f32),
        in_specs=[pl.BlockSpec(memory_space=pltpu.HBM)] * 6,
        out_specs=vmem,
        scratch_shapes=[
            *[pltpu.SMEM(x.shape, jnp.int32) for x in (a_pos, a_num, b_pos, b_num)],
            pltpu.VMEM(a_vals.shape, f32),
            pltpu.VMEM(b_vals.shape, f32),
            pltpu.VMEM((2, rows, full_rows, depth), f32),
            pltpu.VMEM((2, rows * depth, full_cols), f32),
            pltpu.VMEM((2, layers, 2 * part, rows * depth), jnp.bfloat16),
            pltpu.VMEM((2, 2, rows * depth, full_cols), jnp.bfloat16),
            pltpu.VMEM((3, part, full_cols), f32),
            pltpu.VMEM((2, part, full_cols), f32),
            pltpu.SemaphoreType.DMA((n_copies,)),
            pltpu.SemaphoreType.DMA((n_copies,)),
            pltpu.SemaphoreType.DMA((6,)),
        ],
        compiler_params=pltpu.CompilerParams(collective_id=0, has_side_effects=True, vmem_limit_bytes=63 * 2**20),
    )(a_pos, a_num, b_pos, b_num, a_vals, b_vals)


def solution(mesh):
    in_specs = (
        P("row", "col", "layer", None, None, None, None),
        P("row", "col", "layer", None, None, None),
        P("row", "col", "layer", None),
        P("row", "col", "layer", None, None, None),
        P("row", "col", "layer", None, None),
        P("row", "col", "layer"),
    )
    out_specs = P(("row", "layer"), "col")
    call = functools.partial(body, mesh.shape["row"], mesh.shape["col"])
    return jax.shard_map(call, mesh=mesh, in_specs=in_specs, out_specs=out_specs, check_vma=False)
```

```python
import functools

import jax
import jax.numpy as jnp
from jax import lax
from jax.experimental import pallas as pl
from jax.experimental.pallas import tpu as pltpu
from jax.sharding import PartitionSpec as P

MESH = pl.DeviceIdType.MESH
TILE_ROWS = 8
CHUNKS = 4


def inverse(spots, total, bits):
    each = 32 // bits
    words = [jnp.int32(0)] * (-(-total // each))
    for s, spot in enumerate(spots):
        mark = jnp.left_shift(jnp.int32(s + 1), bits * (spot % each))
        for w in range(len(words)):
            inside = jnp.logical_and(spot >= w * each, spot < (w + 1) * each)
            words[w] = words[w] + jnp.where(inside, mark, 0)
    return [jnp.right_shift(words[t // each], bits * (t % each)) & (2**bits - 1) for t in range(total)]


def halves(x):
    high = x.astype(jnp.bfloat16)
    return high, (x - high.astype(jnp.float32)).astype(jnp.bfloat16)


def powers(n):
    out, b = [], n // 2
    while b:
        out.append(b)
        b //= 2
    return out


def multiply(rows, cols, part, depth, n_copies, *refs):
    hbm, out_ref, held = refs[:6], refs[6], refs[7:13]
    a_pos, a_num, b_pos, b_num, a_val, b_val = held
    a_full, b_full, a_half, b_half, sent, landed, send_sem, recv_sem, local_sem = refs[13:]
    i, j, l = lax.axis_index("row"), lax.axis_index("col"), lax.axis_index("layer")
    row_bits, col_bits = powers(rows), powers(cols)
    slots = rows // cols
    width = b_full.shape[3]
    partner = l + 1 - 2 * (l % 2)
    is_inner = jnp.logical_or(l == 1, l == 2)
    is_outer = jnp.logical_or(l == 0, l == 3)
    inner_dest = 1 + l // 2
    outer_dest = 3 * (l // 2)
    dests = [3 - 3 * (l // 2), 2 - l // 2, outer_dest, inner_dest]
    starts = [pl.multiple_of(part * dest, part) for dest in dests]
    near_lo = pl.multiple_of(2 * part * (l // 2), 2 * part)

    def flip(x, bit):
        return x + bit - 2 * bit * ((x // bit) % 2)

    ids = iter(range(n_copies))
    pending = []

    def copy(src, dst, device, back=0):
        k = next(ids)
        return pltpu.make_async_remote_copy(
            src_ref=src, dst_ref=dst, send_sem=send_sem.at[k], recv_sem=recv_sem.at[k - back],
            device_id=device, device_id_type=MESH)

    def when(cond, act):
        if cond is None:
            act()
        else:
            pl.when(cond)(act)

    def start(copies, cond=None):
        when(cond, lambda: [c.start() for c in copies] and None)
        pending.append((copies, cond))

    def arrive(copies, cond=None):
        when(cond, lambda: [c.wait_recv() for c in copies] and None)

    def depart(copies, cond):
        pending[:] = [p for p in pending if p[0] is not copies or p[1] is not cond]
        when(cond, lambda: [c.wait_send() for c in copies] and None)

    def at(piece):
        return pl.ds(pl.multiple_of(piece * depth, depth), depth)

    def b_view(q, piece, c):
        return b_full.at[q, c, at(piece)]

    def b_stage(q, c, stage):
        bit = row_bits[stage]
        offsets = [0]
        for b in row_bits[:stage]:
            offsets = offsets + [o + b for o in offsets]
        copies = []
        for o in offsets:
            owner = i
            for b in row_bits[:stage]:
                if o & b:
                    owner = flip(owner, b)
            piece = (owner + j) % rows
            src = b_view(q, piece, c)
            copies.append(copy(src, b_view(q, piece, c), {"row": flip(i, bit)}))
        return copies

    def a_view(q, lo, size, piece):
        return a_full.at[q, piece, pl.ds(lo, size)]

    def a_stage(q, lo, size, stage):
        bit = col_bits[stage]
        owners = [j]
        for b in col_bits[:stage]:
            owners = owners + [flip(o, b) for o in owners]
        copies = []
        for o in owners:
            for m in range(slots):
                piece = (i + o + cols * m) % rows
                src = a_view(q, lo, size, piece)
                copies.append(copy(src, a_view(q, lo, size, piece), {"col": flip(j, bit)}))
        return copies

    my_pieces = [(i + j + cols * m) % rows for m in range(slots)]
    to_partner = {"layer": partner}

    def z_a(lo, size):
        return [copy(a_view(0, lo, size, my_pieces[m]),
                     a_view(1, lo, size, my_pieces[m]), to_partner) for m in range(slots)]

    def z_b(c):
        return [copy(b_view(0, my_pieces[0], c), b_view(1, my_pieces[0], c), to_partner)]

    loads = [pltpu.make_async_copy(src, dst, local_sem.at[n]) for n, (src, dst) in enumerate(zip(hbm, held))]
    for load in loads:
        load.start()

    barrier = pltpu.get_barrier_semaphore()
    peers = [{"row": flip(i, b)} for b in row_bits] + [{"col": flip(j, b)} for b in col_bits]
    peers += [{"layer": (l + d) % 4} for d in (1, 2, 3)]
    for peer in peers:
        pl.semaphore_signal(barrier, inc=1, device_id=peer, device_id_type=MESH)

    for load in loads[:4]:
        load.wait()

    block = a_val.shape[-1]
    inner, tile_cols = depth // block, CHUNKS * width // block
    caps = a_val.shape[1]
    a_slot = [
        inverse([jnp.where(s < a_num[m], a_pos[m, 0, s] * inner + a_pos[m, 1, s], -1) for s in range(caps)],
                TILE_ROWS * inner, 4)
        for m in range(slots)
    ]
    b_slot = inverse(
        [jnp.where(s < b_num[0], b_pos[0, s] * tile_cols + b_pos[1, s], -1) for s in range(b_val.shape[0])],
        inner * tile_cols, 8)

    def stored(ref, slot):
        value = ref[jnp.maximum(slot - 1, 0)]
        return jnp.where(slot > 0, value, jnp.zeros_like(value))

    def a_dense():
        for m in range(slots):
            for r in range(TILE_ROWS):
                parts = [stored(a_val.at[m], a_slot[m][r * inner + k]) for k in range(inner)]
                a_full[0, my_pieces[m], pl.ds(r * block, block)] = jnp.concatenate(parts, 1)

    def b_dense(c):
        for r in range(inner):
            rows_r = pl.ds(pl.multiple_of(my_pieces[0] * depth + r * block, block), block)
            for k in range(c * width // block, (c + 1) * width // block, 2):
                parts = [stored(b_val, b_slot[r * tile_cols + k + d]) for d in range(2)]
                b_full[0, c, rows_r, pl.ds(k * block - c * width, 2 * block)] = jnp.concatenate(parts, 1)

    for load in loads[4:]:
        load.wait()
    a_dense()
    b_dense(0)
    b_dense(1)
    pl.semaphore_wait(barrier, len(peers))

    def a_finish(q, lo, size, first, cond):
        arrive(first, cond)
        for stage in range(1, len(col_bits)):
            more = a_stage(q, lo, size, stage)
            start(more, cond)
            arrive(more, cond)

    def b_relay(q, c, first, cond):
        arrive(first, cond)
        for stage in range(1, len(row_bits)):
            more = b_stage(q, c, stage)
            start(more, cond)
            if stage < len(row_bits) - 1:
                arrive(more, cond)
        return more

    step = min(rows * depth, 512)

    def steps(act):
        total = rows * depth // step
        if total == 1:
            act(pl.ds(0, step))
        else:
            pl.loop(0, total)(lambda k: act(pl.ds(pl.multiple_of(k * step, step), step)))

    def chunk(c):
        return pl.ds(c * width, width)

    def halve_a(q, n):
        def act(piece):
            k = at(piece)
            high, low = halves(a_full[q, piece, pl.ds(starts[n], part)])
            a_half[q, n, pl.ds(0, part), k] = high
            a_half[q, n, pl.ds(part, part), k] = low
        if rows <= 4:
            for piece in range(rows):
                act(piece)
        else:
            pl.loop(0, rows)(act)

    def halve_b(q, c):
        def act(k):
            b_half[q, 0, c, k], b_half[q, 1, c, k] = halves(b_full[q, c, k])
        steps(act)

    def product(layers, n, c, out):
        def term(q, k):
            first = jnp.dot(a_half[q, n, :, k], b_half[q, 0, c, k], preferred_element_type=jnp.float32)
            other = jnp.dot(a_half[q, n, pl.ds(0, part), k], b_half[q, 1, c, k], preferred_element_type=jnp.float32)
            return first[:part] + (first[part:] + other)

        if rows * depth == step:
            value = term(layers[0], pl.ds(0, step))
            for q in layers[1:]:
                value = value + term(q, pl.ds(0, step))
            out[...] = value
        else:
            out[...] = jnp.zeros((part, width), jnp.float32)
            for q in layers:
                def act(k, q=q):
                    out[...] += term(q, k)
                steps(act)

    far_sent, near_sent = [], []
    for c in range(CHUNKS):
        far_sent.append([copy(sent.at[n, c], landed.at[0, c], {"layer": dests[n]}, n) for n in range(2)])
        near_sent.append([copy(sent.at[2, c], landed.at[1, c], to_partner)])

    def far_chunk(n, c):
        when(is_inner, lambda: product((0, 1), n, c, sent.at[n, c]))
        start([far_sent[c][n]], is_inner)

    def near_chunk(c):
        when(is_inner, lambda: product((0,), 2, c, sent.at[2, c]))
        start(near_sent[c], is_inner)

    def chunk_here(c):
        arrive(last0[c])
        arrive(last1[c], is_inner)
        halve_b(0, c)
        when(is_inner, lambda: halve_b(1, c))

    def outer_chunk(c):
        when(is_outer, lambda: product((0,), 2, c, out_ref.at[:, chunk(c)]))

    za = [z_a(starts[n], part) for n in (0, 1, 3)]
    zb = [z_b(c) for c in range(CHUNKS)]
    fo0, fi0 = a_stage(0, starts[0], part, 0), a_stage(0, starts[1], part, 0)
    fo1, fi1 = a_stage(1, starts[0], part, 0), a_stage(1, starts[1], part, 0)
    near0, inner1 = a_stage(0, near_lo, 2 * part, 0), a_stage(1, starts[3], part, 0)
    b0 = [b_stage(0, c, 0) for c in range(CHUNKS)]
    b1 = [b_stage(1, c, 0) for c in range(CHUNKS)]
    last0, last1 = [None] * CHUNKS, [None] * CHUNKS

    start(za[0], is_outer)
    start(fo0, is_inner)
    start(b0[0])
    start(zb[0], is_outer)
    start(za[1], is_outer)
    start(near0, is_outer)
    start(b0[1])
    for c in range(2, CHUNKS):
        b_dense(c)
    last0[0] = b_relay(0, 0, b0[0], None)
    arrive(za[0], is_inner)
    start(fo1, is_inner)
    start(fi0, is_inner)
    start(b0[2])
    depart(za[0], is_outer)
    start(zb[1], is_outer)
    arrive(zb[0], is_inner)
    start(b1[0], is_inner)
    depart(zb[0], is_outer)
    start(zb[2], is_outer)
    last0[1] = b_relay(0, 1, b0[1], None)
    start(b0[3])
    a_finish(0, starts[0], part, fo0, is_inner)
    a_finish(1, starts[0], part, fo1, is_inner)
    when(is_inner, lambda: [halve_a(q, 0) for q in range(2)] and None)
    last1[0] = b_relay(1, 0, b1[0], is_inner)
    arrive(za[1], is_inner)
    start(fi1, is_inner)
    start(near0, is_inner)
    depart(za[1], is_outer)
    start(zb[3], is_outer)
    chunk_here(0)
    far_chunk(0, 0)
    arrive(zb[1], is_inner)
    start(b1[1], is_inner)
    depart(zb[1], is_outer)
    start(za[2], is_outer)
    a_finish(0, starts[1], part, fi0, is_inner)
    a_finish(1, starts[1], part, fi1, is_inner)
    when(is_inner, lambda: [halve_a(q, 1) for q in range(2)] and None)
    far_chunk(1, 0)
    last0[2] = b_relay(0, 2, b0[2], None)
    arrive(zb[2], is_inner)
    start(b1[2], is_inner)
    last1[1] = b_relay(1, 1, b1[1], is_inner)
    chunk_here(1)
    far_chunk(0, 1)
    far_chunk(1, 1)
    arrive(zb[3], is_inner)
    start(b1[3], is_inner)
    a_finish(0, near_lo, 2 * part, near0, None)
    halve_a(0, 2)
    when(is_inner, lambda: halve_a(0, 3))
    near_chunk(0)
    outer_chunk(0)
    outer_chunk(1)
    last0[3] = b_relay(0, 3, b0[3], None)
    last1[2] = b_relay(1, 2, b1[2], is_inner)
    chunk_here(2)
    far_chunk(0, 2)
    far_chunk(1, 2)
    near_chunk(1)
    outer_chunk(2)
    arrive(za[2], is_inner)
    start(inner1, is_inner)
    last1[3] = b_relay(1, 3, b1[3], is_inner)
    chunk_here(3)
    far_chunk(0, 3)
    far_chunk(1, 3)
    near_chunk(2)
    near_chunk(3)
    outer_chunk(3)
    a_finish(1, starts[3], part, inner1, is_inner)
    when(is_inner, lambda: halve_a(1, 3))
    for c in range(CHUNKS):
        when(is_inner, lambda c=c: product((0, 1), 3, c, out_ref.at[:, chunk(c)]))
    for c in range(CHUNKS):
        far_sent[c][0].wait_recv()
        out_ref[:, chunk(c)] += landed[0, c]

        def add(c=c):
            near_sent[c][0].wait_recv()
            out_ref[:, chunk(c)] += landed[1, c]
        when(is_outer, add)
    for copies, cond in list(pending):
        depart(copies, cond)


def body(rows, cols, a_values, a_places, a_counts, b_values, b_places, b_counts):
    a_vals = a_values.reshape(a_values.shape[3:])
    b_vals = b_values.reshape(b_values.shape[3:])
    slots, block = a_vals.shape[0], a_vals.shape[2]
    layers = lax.axis_size("layer")
    inner = TILE_ROWS // layers
    tile_cols = TILE_ROWS * rows // cols
    a_pos = jnp.swapaxes(a_places.reshape(a_places.shape[3:]), 1, 2)
    a_num = a_counts.reshape(slots)
    b_pos = b_places.reshape(b_places.shape[3:]).T
    b_num = b_counts.reshape(1)
    depth, part = inner * block, TILE_ROWS * block // layers
    full_rows, full_cols = TILE_ROWS * block, tile_cols * block
    width = full_cols // CHUNKS
    f32 = jnp.float32
    vmem = pl.BlockSpec(memory_space=pltpu.VMEM)
    n_copies = 2 * CHUNKS * (rows - 1) + 6 * slots * (cols - 1) + 3 * slots + 4 * CHUNKS
    return pl.pallas_call(
        functools.partial(multiply, rows, cols, part, depth, n_copies),
        out_shape=jax.ShapeDtypeStruct((part, full_cols), f32),
        in_specs=[pl.BlockSpec(memory_space=pltpu.HBM)] * 6,
        out_specs=vmem,
        scratch_shapes=[
            *[pltpu.SMEM(x.shape, jnp.int32) for x in (a_pos, a_num, b_pos, b_num)],
            pltpu.VMEM(a_vals.shape, f32),
            pltpu.VMEM(b_vals.shape, f32),
            pltpu.VMEM((2, rows, full_rows, depth), f32),
            pltpu.VMEM((2, CHUNKS, rows * depth, width), f32),
            pltpu.VMEM((2, layers, 2 * part, rows * depth), jnp.bfloat16),
            pltpu.VMEM((2, 2, CHUNKS, rows * depth, width), jnp.bfloat16),
            pltpu.VMEM((3, CHUNKS, part, width), f32),
            pltpu.VMEM((2, CHUNKS, part, width), f32),
            pltpu.SemaphoreType.DMA((n_copies,)),
            pltpu.SemaphoreType.DMA((n_copies,)),
            pltpu.SemaphoreType.DMA((6,)),
        ],
        compiler_params=pltpu.CompilerParams(collective_id=0, has_side_effects=True, vmem_limit_bytes=63 * 2**20),
    )(a_pos, a_num, b_pos, b_num, a_vals, b_vals)


def solution(mesh):
    in_specs = (
        P("row", "col", "layer", None, None, None, None),
        P("row", "col", "layer", None, None, None),
        P("row", "col", "layer", None),
        P("row", "col", "layer", None, None, None),
        P("row", "col", "layer", None, None),
        P("row", "col", "layer"),
    )
    out_specs = P(("row", "layer"), "col")
    call = functools.partial(body, mesh.shape["row"], mesh.shape["col"])
    return jax.shard_map(call, mesh=mesh, in_specs=in_specs, out_specs=out_specs, check_vma=False)
```
